256 devices in a mesh: slab: 64 (over y, z, core), batch: 4 (over x).
Axes of the slice: x: 4, y: 4, z: 8, core: 2. Of those that a mesh axis runs over, the one named last changes fastest.
Arguments:
- fields: bfloat16 [4, 32, 256, 128, 128], P('batch', None, 'slab'), may hold values from -6 to 6
- cotangent: bfloat16 [4, 32, 256, 128, 128], P('batch', None, 'slab'), may hold values from -6 to 6
- local_weight: bfloat16 [32, 32], replicated, may hold values from -1 to 1
- spectral_weight: bfloat16 [2, 32, 32, 16384], P(None, None, None, ('slab', 'batch')), may hold values from -4 to 4
Outputs:
- field_grad: bfloat16 [4, 32, 256, 128, 128], P('batch', None, 'slab')
- weight_grad: float32 [2, 32, 32, 16384], P(None, None, None, ('slab', 'batch'))
The draws below stay inside these ranges and needn't reach their ends.
All inputs are finite; a program needn't handle non-finite values.
Results may differ from the reference program's by a relative error of at most 0.023.
Values may be sent and summed in bfloat16 or wider, within the bound.
A program may use at most 128 MiB of HBM per device.

```python
import math
from functools import partial
import jax
import jax.numpy as jnp
from jax import lax

C = 32
NY = 128
NZ = 128
MX = 32
MY = 32
MZ = 16
NX = 256
SAMPLES = 4
MODES = 16384


def level_of(own_key, dims, cuts, smallest, high):
    gain = 1.0
    for axis_at, blocks in cuts:
        heights = jax.random.uniform(jax.random.fold_in(jax.random.fold_in(own_key, 6), axis_at), (blocks,), jnp.float32, smallest / len(cuts), high / len(cuts))
        gain = gain * jnp.repeat(jnp.exp(heights), dims[axis_at] // blocks).reshape((-1,) + (1,) * (len(dims) - 1 - axis_at))
    return gain


def normal_values(rng, extent, scale, limit, cuts=(), held_as=jnp.bfloat16):
    values = jax.random.normal(rng, extent, jnp.float32) * scale
    if len(cuts) > 0:
        values = level_of(rng, extent, cuts, -0.22, 0.18) * values
    return jnp.clip(values, min=-limit, max=limit).astype(held_as)


def setup_inputs(seed: int = 0) -> dict:
    key_list = jax.random.split(jax.random.key(seed), 5)
    fields = normal_values(key_list[0], (SAMPLES, C, NX, NY, NZ), 1.0, 6.0, ((0, 4), (2, 64)))
    cotangent = normal_values(key_list[1], (SAMPLES, C, NX, NY, NZ), 1.0, 6.0, ((0, 4), (2, 64)))
    local_weight = normal_values(key_list[2], (C, C), C ** -0.5, 1.0)
    spectral_weight = normal_values(key_list[3], (2, C, C, MODES), 1.0, 4.0, ((3, 256),))
    return dict(fields=fields, cotangent=cotangent, local_weight=local_weight, spectral_weight=spectral_weight)


def frequencies(number, signed):
    counter = jnp.arange(number, dtype=jnp.int32)
    if signed:
        return jnp.where(counter < number // 2, counter, counter - number)
    return counter

def wave_table(number, length, signed):
    wave_numbers = frequencies(number, signed)
    positions = jnp.arange(length, dtype=jnp.int32)
    phases = jnp.mod(wave_numbers[:, None] * positions[None, :], length).astype(jnp.float32)
    angles = phases * (2.0 * math.pi / length)
    return (jnp.cos(angles), jnp.sin(angles))

def forward_pair(cos_table, sin_table):
    cos_rows = cos_table.T
    sin_rows = sin_table.T
    return jnp.stack([jnp.stack([cos_rows, -sin_rows], 1), jnp.stack([sin_rows, cos_rows], 1)], 1).astype(jnp.bfloat16)

def inverse_pair(cos_table, sin_table):
    return jnp.stack([jnp.stack([cos_table, sin_table], 1), jnp.stack([-sin_table, cos_table], 1)], 1).astype(jnp.bfloat16)

def make_tables(length_x):
    cos_y, sin_y = wave_table(MY, NY, True)
    cos_z, sin_z = wave_table(MZ, NZ, False)
    cos_x, sin_x = wave_table(MX, length_x, True)
    analysis_y = jnp.stack([cos_y.T, -sin_y.T], 1).astype(jnp.bfloat16)
    final_y = jnp.stack([cos_y, -sin_y], 0).astype(jnp.bfloat16)
    return (analysis_y, forward_pair(cos_z, sin_z), forward_pair(cos_x, sin_x), inverse_pair(cos_x, sin_x), inverse_pair(cos_z, sin_z), final_y)

def wide(array):
    return array.astype(jnp.float32)

def analyse_whole(field, tables):
    analysis_y, pair_z, pair_x = (tables[0], tables[1], tables[2])

    def one_channel(plane):
        first = jnp.einsum('xyz,ypk->xpkz', wide(plane), wide(analysis_y)).astype(jnp.bfloat16)
        second = jnp.einsum('xpyz,zpqk->xqyk', wide(first), wide(pair_z)).astype(jnp.bfloat16)
        second = second.reshape(NX, 2, MY * MZ)
        third = jnp.einsum('xpm,xpqk->qmk', wide(second), wide(pair_x))
        return third.reshape(2, MODES)
    return lax.map(one_channel, field)

def synthesise_whole(spectra, tables):
    back_x, back_z, final_y = (tables[3], tables[4], tables[5])

    def one_channel(spectrum):
        grid = spectrum.reshape(2, MY * MZ, MX)
        first = jnp.einsum('pmk,kpqx->xqm', wide(grid), wide(back_x)).astype(jnp.bfloat16)
        first = first.reshape(NX, 2, MY, MZ)
        second = jnp.einsum('xpyk,kpqz->xqyz', wide(first), wide(back_z)).astype(jnp.bfloat16)
        return jnp.einsum('xpkz,pky->xyz', wide(second), wide(final_y))
    return lax.map(one_channel, spectra)

def spectral_mix(values, weights):
    product = partial(jnp.einsum, precision=lax.Precision.HIGHEST)
    real_w = wide(weights[0])
    imag_w = wide(weights[1])
    real_v = values[:, :, 0]
    imag_v = values[:, :, 1]
    out_real = product('sck,cok->sok', real_v, real_w) - product('sck,cok->sok', imag_v, imag_w)
    out_imag = product('sck,cok->sok', imag_v, real_w) + product('sck,cok->sok', real_v, imag_w)
    return jnp.stack([out_real, out_imag], 2).astype(jnp.bfloat16)

def spectral_adjoint(grads, values, weights):
    product = partial(jnp.einsum, precision=lax.Precision.HIGHEST)
    real_w = wide(weights[0])
    imag_w = wide(weights[1])
    real_g = grads[:, :, 0]
    imag_g = grads[:, :, 1]
    real_v = values[:, :, 0]
    imag_v = values[:, :, 1]
    grad_real = product('sok,sck->cok', real_g, real_v) + product('sok,sck->cok', imag_g, imag_v)
    grad_imag = product('sok,sck->cok', imag_g, real_v) - product('sok,sck->cok', real_g, imag_v)
    back_real = product('cok,sok->sck', real_w, real_g) + product('cok,sok->sck', imag_w, imag_g)
    back_imag = product('cok,sok->sck', real_w, imag_g) - product('cok,sok->sck', imag_w, real_g)
    return (jnp.stack([grad_real, grad_imag], 0), jnp.stack([back_real, back_imag], 2).astype(jnp.bfloat16))

def gelu_slope(values):
    normal_cdf = 0.5 * (1.0 + jax.scipy.special.erf(values / math.sqrt(2.0)))
    density = jnp.exp(-0.5 * values * values) / math.sqrt(2.0 * math.pi)
    return normal_cdf + values * density

def reference(fields, cotangent, local_weight, spectral_weight):
    tables = make_tables(NX)
    scale_in = 1.0 / math.sqrt(NX * NY * NZ)
    scale_out = 1.0 / math.sqrt(MODES * C)

    def per_sample(running, sample):
        field, upstream = sample
        spectrum = analyse_whole(field, tables) * scale_in
        mixed_modes = spectral_mix(spectrum[None], spectral_weight)[0]
        kernel_part = synthesise_whole(mixed_modes, tables) * scale_out
        linear = jnp.einsum('cxyz,co->oxyz', wide(field), wide(local_weight))
        slope_grad = (wide(upstream) * gelu_slope(linear + kernel_part)).astype(jnp.bfloat16)
        grad_modes = analyse_whole(slope_grad, tables) * scale_out
        weight_part, back_modes = spectral_adjoint(grad_modes[None], spectrum[None], spectral_weight)
        through = jnp.einsum('oxyz,co->cxyz', wide(slope_grad), wide(local_weight))
        field_grad = (through + synthesise_whole(back_modes[0], tables) * scale_in).astype(jnp.bfloat16)
        return (running + weight_part, field_grad)
    initial = jnp.zeros((2, C, C, MODES), jnp.float32)
    weight_grad, field_grad = lax.scan(per_sample, initial, (fields, cotangent))
    return (field_grad, weight_grad)
```

```python
from functools import partial
import math

import jax
import jax.numpy as jnp
from jax import lax
from jax.experimental import pallas as pl
from jax.experimental.pallas import tpu as pltpu
from jax.sharding import PartitionSpec as P

C = 32
NY = 128
NZ = 128
MX = 32
MY = 32
MZ = 16
MESH = pl.DeviceIdType.MESH


def frequencies(number, signed):
    counter = jnp.arange(number, dtype=jnp.int32)
    if signed:
        return jnp.where(counter < number // 2, counter, counter - number)
    return counter


def wave_table(number, length, signed):
    wave_numbers = frequencies(number, signed)
    positions = jnp.arange(length, dtype=jnp.int32)
    phases = jnp.mod(wave_numbers[:, None] * positions[None, :], length).astype(jnp.float32)
    angles = phases * (2.0 * math.pi / length)
    return (jnp.cos(angles), jnp.sin(angles))


def forward_pair(cos_table, sin_table):
    cos_rows = cos_table.T
    sin_rows = sin_table.T
    return jnp.stack(
        [jnp.stack([cos_rows, -sin_rows], 1), jnp.stack([sin_rows, cos_rows], 1)], 1
    ).astype(jnp.bfloat16)


def inverse_pair(cos_table, sin_table):
    return jnp.stack(
        [jnp.stack([cos_table, sin_table], 1), jnp.stack([-sin_table, cos_table], 1)], 1
    ).astype(jnp.bfloat16)


def make_tables(length_x):
    cos_y, sin_y = wave_table(MY, NY, True)
    cos_z, sin_z = wave_table(MZ, NZ, False)
    cos_x, sin_x = wave_table(MX, length_x, True)
    analysis_y = jnp.stack([cos_y.T, -sin_y.T], 1).astype(jnp.bfloat16)
    final_y = jnp.stack([cos_y, -sin_y], 0).astype(jnp.bfloat16)
    return (
        analysis_y,
        forward_pair(cos_z, sin_z),
        forward_pair(cos_x, sin_x),
        inverse_pair(cos_x, sin_x),
        inverse_pair(cos_z, sin_z),
        final_y,
    )


def contract(formula, left, right):
    return jnp.einsum(formula, left, right, preferred_element_type=jnp.float32)


def exchange_kernel(slabs, batches, src, dst, send_sem, recv_sem, own_sem):
    count = slabs * batches
    me = lax.axis_index("slab") * batches + lax.axis_index("batch")

    def place(index):
        return (index // batches, index % batches)

    barrier = pltpu.get_barrier_semaphore()

    def greet(step, carry):
        pl.semaphore_signal(
            barrier, inc=1, device_id=place((me + step) % count), device_id_type=MESH
        )
        return carry

    lax.fori_loop(1, count, greet, 0)
    pl.semaphore_wait(barrier, count - 1)

    def send(step, carry):
        target = (me + step) % count
        pltpu.make_async_remote_copy(
            src_ref=src.at[target],
            dst_ref=dst.at[me],
            send_sem=send_sem,
            recv_sem=recv_sem,
            device_id=place(target),
            device_id_type=MESH,
        ).start()
        return carry

    lax.fori_loop(1, count, send, 0)
    own = pltpu.make_async_copy(src.at[me], dst.at[me], own_sem)
    own.start()
    own.wait()
    some = pl.ds(0, count - 1)
    pltpu.make_async_copy(src.at[some], dst.at[some], send_sem).wait()
    pltpu.make_async_copy(src.at[some], dst.at[some], recv_sem).wait()


def exchange(messages):
    slabs, batches = lax.axis_size("slab"), lax.axis_size("batch")
    return pl.pallas_call(
        partial(exchange_kernel, slabs, batches),
        out_shape=jax.ShapeDtypeStruct(messages.shape, messages.dtype),
        in_specs=[pl.BlockSpec(memory_space=pltpu.VMEM)],
        out_specs=pl.BlockSpec(memory_space=pltpu.VMEM),
        scratch_shapes=[pltpu.SemaphoreType.DMA] * 3,
        compiler_params=pltpu.CompilerParams(collective_id=0, has_side_effects=True),
    )(messages)


def analyse(field, tables):
    analysis_y, pair_z, pair_x = (tables[0], tables[1], tables[2])
    first = contract("bcxyz,ypk->bcxpkz", field, analysis_y).astype(jnp.bfloat16)
    second = contract("bcxpyz,zpqk->bcxqyk", first, pair_z).astype(jnp.bfloat16)
    channels, width_x = second.shape[1], second.shape[2]
    slabs, batches = lax.axis_size("slab"), lax.axis_size("batch")
    devices = slabs * batches
    held = MY * MZ // devices
    second = second.reshape(channels, width_x, 2, devices, held)
    messages = jnp.transpose(second, (3, 1, 2, 4, 0)).reshape(devices, width_x, 2 * held * channels)
    got = exchange(messages).reshape(slabs, batches, width_x, 2, held, channels)
    table = pair_x.reshape(slabs, width_x, 2, 2, MX)
    return contract("wsxpbc,wxpqk->scqbk", got, table).reshape(batches, channels, 2, held * MX)


def synthesise(modes_part, tables, width_x):
    back_x, back_z, final_y = (tables[3], tables[4], tables[5])
    samples, channels = (modes_part.shape[0], modes_part.shape[1])
    slabs, batches = lax.axis_size("slab"), lax.axis_size("batch")
    devices = slabs * batches
    held = MY * MZ // devices
    grid = modes_part.reshape(samples, channels, 2, held, MX)
    columns = back_x.reshape(MX, 2, 2, slabs, width_x)
    first = contract("scpbk,kpqwx->wsxqbc", grid, columns).astype(jnp.bfloat16)
    messages = first.reshape(devices, width_x, 2 * held * channels)
    got = exchange(messages).reshape(MY, MZ // held, width_x, 2, held, channels)
    first = jnp.transpose(got, (5, 2, 3, 0, 1, 4)).reshape(1, channels, width_x, 2, MY, MZ)
    second = contract("bcxpyk,kpqz->bcxqyz", first, back_z).astype(jnp.bfloat16)
    return contract("bcxpkz,pky->bcxyz", second, final_y)


def spectral_mix(values, weights):
    product = partial(jnp.einsum, precision=lax.Precision.HIGHEST)
    real_w = weights[0].astype(jnp.float32)
    imag_w = weights[1].astype(jnp.float32)
    real_v = values[:, :, 0]
    imag_v = values[:, :, 1]
    out_real = product("sck,cok->sok", real_v, real_w) - product("sck,cok->sok", imag_v, imag_w)
    out_imag = product("sck,cok->sok", imag_v, real_w) + product("sck,cok->sok", real_v, imag_w)
    return jnp.stack([out_real, out_imag], 2).astype(jnp.bfloat16)


def spectral_adjoint(grads, values, weights):
    product = partial(jnp.einsum, precision=lax.Precision.HIGHEST)
    real_w = weights[0].astype(jnp.float32)
    imag_w = weights[1].astype(jnp.float32)
    real_g = grads[:, :, 0]
    imag_g = grads[:, :, 1]
    real_v = values[:, :, 0]
    imag_v = values[:, :, 1]
    grad_real = product("sok,sck->cok", real_g, real_v) + product("sok,sck->cok", imag_g, imag_v)
    grad_imag = product("sok,sck->cok", imag_g, real_v) - product("sok,sck->cok", real_g, imag_v)
    back_real = product("cok,sok->sck", real_w, real_g) + product("cok,sok->sck", imag_w, imag_g)
    back_imag = product("cok,sok->sck", real_w, imag_g) - product("cok,sok->sck", imag_w, real_g)
    return (
        jnp.stack([grad_real, grad_imag], 0),
        jnp.stack([back_real, back_imag], 2).astype(jnp.bfloat16),
    )


def gelu_slope(values):
    normal_cdf = 0.5 * (1.0 + jax.scipy.special.erf(values / math.sqrt(2.0)))
    density = jnp.exp(-0.5 * values * values) / math.sqrt(2.0 * math.pi)
    return normal_cdf + values * density


def body(fields, cotangent, local_weight, spectral_weight):
    width_x = fields.shape[2]
    length_x = width_x * lax.axis_size("slab")
    tables = make_tables(length_x)
    scale_in = 1.0 / math.sqrt(length_x * NY * NZ)
    scale_out = 1.0 / math.sqrt(MX * MY * MZ * C)
    spectrum = analyse(fields, tables) * scale_in
    mixed_modes = spectral_mix(spectrum, spectral_weight)
    kernel_part = synthesise(mixed_modes, tables, width_x) * scale_out
    linear = contract("bcxyz,co->boxyz", fields, local_weight)
    slope_grad = (cotangent.astype(jnp.float32) * gelu_slope(linear + kernel_part)).astype(
        jnp.bfloat16
    )
    grad_modes = analyse(slope_grad, tables) * scale_out
    weight_grad, back_modes = spectral_adjoint(grad_modes, spectrum, spectral_weight)
    through = contract("boxyz,co->bcxyz", slope_grad, local_weight)
    field_grad = (through + synthesise(back_modes, tables, width_x) * scale_in).astype(
        jnp.bfloat16
    )
    return (field_grad, weight_grad)


def solution(mesh):
    placed = (
        P("batch", None, "slab", None, None),
        P("batch", None, "slab", None, None),
        P(),
        P(None, None, None, ("slab", "batch")),
    )
    return jax.shard_map(
        body,
        mesh=mesh,
        in_specs=placed,
        out_specs=(P("batch", None, "slab", None, None), P(None, None, None, ("slab", "batch"))),
        check_vma=False,
    )
```

```python
from functools import partial
import math

import jax
import jax.numpy as jnp
import ml_dtypes
import numpy as np
from jax import lax
from jax.experimental import pallas as pl
from jax.experimental.pallas import tpu as pltpu
from jax.sharding import PartitionSpec as P

C = 32
NX = 256
NY = 128
NZ = 128
MX = 32
MY = 32
MZ = 16
SLABS = 64
BATCHES = 4
DEVICES = SLABS * BATCHES
WIDTH = NX // SLABS
HELD = MY * MZ // DEVICES
HIGH = MZ // HELD
GROUP = 8
GROUPS = C // GROUP
BAND = 16
MESH = pl.DeviceIdType.MESH
F32 = jnp.float32
BF16 = jnp.bfloat16
SCALE_IN = 1.0 / math.sqrt(NX * NY * NZ)
SCALE_OUT = 1.0 / math.sqrt(MX * MY * MZ * C)


def wave_table(number, length, signed):
    numbers = np.arange(number)
    if signed:
        numbers = np.where(numbers < number // 2, numbers, numbers - number)
    phases = np.mod(numbers[:, None] * np.arange(length)[None, :], length).astype(np.float32)
    angles = phases * np.float32(2.0 * math.pi / length)
    return (np.cos(angles).astype(np.float32), np.sin(angles).astype(np.float32))


def make_tables():
    cos_y, sin_y = wave_table(MY, NY, True)
    cos_z, sin_z = wave_table(MZ, NZ, False)
    cos_x, sin_x = wave_table(MX, NX, True)
    eye = np.eye(GROUP, dtype=np.float32)
    pair_y = np.stack([cos_y, -sin_y])
    analysis_y = np.einsum("pky,ab->pkaby", pair_y, eye).reshape(2 * MY * GROUP, GROUP * NY)
    synthesis_y = np.einsum("pky,ab->aypkb", pair_y, eye).reshape(GROUP * NY, 2 * MY * GROUP)
    analysis_z = np.stack([np.stack([cos_z, sin_z], 1), np.stack([-sin_z, cos_z], 1)])
    analysis_z = analysis_z.reshape(2, HIGH, HELD, 2 * NZ).transpose(1, 0, 2, 3).reshape(2 * MZ, 2 * NZ)
    synthesis_z = np.stack([np.stack([cos_z, sin_z], 1), np.stack([-sin_z, cos_z], 1)])
    synthesis_z = synthesis_z.reshape(2, HIGH, HELD, 2 * NZ).transpose(1, 0, 2, 3).reshape(2 * MZ, 2 * NZ)
    both_x = np.stack([cos_x, sin_x]).reshape(2, MX, SLABS, WIDTH).transpose(0, 1, 3, 2)
    analysis_x = both_x.reshape(2 * MX, WIDTH * SLABS)
    synthesis_x = both_x.transpose(3, 2, 0, 1).reshape(SLABS, WIDTH * 2 * MX)
    tables = (analysis_y, synthesis_y, analysis_z, synthesis_z, analysis_x, synthesis_x)
    return tuple(np.ascontiguousarray(table).astype(ml_dtypes.bfloat16) for table in tables)


def matmul(left, right):
    return jnp.dot(left, right, preferred_element_type=F32)


def gelu_slope(values):
    size = jnp.abs(values)
    inverse = 1.0 / (1.0 + (0.3275911 / math.sqrt(2.0)) * size)
    tail = 0.5 * 1.061405429 * inverse - 0.5 * 1.453152027
    tail = tail * inverse + 0.5 * 1.421413741
    tail = tail * inverse - 0.5 * 0.284496736
    tail = tail * inverse + 0.5 * 0.254829592
    tail = tail * inverse - size * (1.0 / math.sqrt(2.0 * math.pi))
    below = jnp.exp(-0.5 * values * values) * tail
    return jnp.where(values >= 0.0, 1.0 - below, below)


def lane_groups(value):
    lanes = lax.broadcasted_iota(jnp.int32, value.shape, 1) // C
    return [jnp.where(lanes == group, value, 0.0) for group in range(WIDTH)]


def spread(weight):
    rows = C * BAND
    left = (
        lax.broadcasted_iota(jnp.int32, (rows, C), 0) // BAND
        == lax.broadcasted_iota(jnp.int32, (rows, C), 1)
    ).astype(F32).astype(BF16)
    right = (
        lax.broadcasted_iota(jnp.int32, (C, rows), 1) // BAND
        == lax.broadcasted_iota(jnp.int32, (C, rows), 0)
    ).astype(F32).astype(BF16)
    whole = matmul(matmul(left, weight).astype(BF16), right)
    same = (
        lax.broadcasted_iota(jnp.int32, (rows, rows), 0) % BAND
        == lax.broadcasted_iota(jnp.int32, (rows, rows), 1) % BAND
    )
    return jnp.where(same, whole, 0.0).astype(BF16)


def kernel(
    fields, cotangent, forward_map, backward_map, weights,
    analysis_y, synthesis_y, analysis_z, synthesis_z, analysis_x, synthesis_x,
    field_grad, weight_grad,
    sent, got, grid, flat, linear, slope, doubled, values, grads, modes, result, spread_map,
    send_sem, recv_sem, own_sem,
):
    me = lax.axis_index("slab") * BATCHES + lax.axis_index("batch")

    def place(index):
        return (index // BATCHES, index % BATCHES)

    barrier = pltpu.get_barrier_semaphore()

    def greet(step, carry):
        pl.semaphore_signal(
            barrier, inc=1, device_id=place((me + step) % DEVICES), device_id_type=MESH
        )
        return carry

    lax.fori_loop(1, DEVICES, greet, 0)

    def send(turn, target):
        @pl.when(target != me)
        def _():
            pltpu.make_async_remote_copy(
                src_ref=sent.at[turn, target],
                dst_ref=got.at[turn, me],
                send_sem=send_sem.at[turn],
                recv_sem=recv_sem.at[turn],
                device_id=place(target),
                device_id_type=MESH,
            ).start()

        @pl.when(target == me)
        def _():
            pltpu.make_async_copy(
                sent.at[turn, me], got.at[turn, me], own_sem.at[turn]
            ).start()

    def receive(turn):
        pltpu.make_async_copy(sent.at[turn, me], got.at[turn, me], own_sem.at[turn]).wait()
        some = pl.ds(0, DEVICES - 1)
        pltpu.make_async_copy(
            sent.at[turn, some], got.at[turn, some], recv_sem.at[turn]
        ).wait()

        def unpack(step, carry):
            for inner in range(8):
                index = step * 8 + inner
                flat[pl.ds(pl.multiple_of(index * 4, 4), 4), :] = got[turn, index].astype(F32)
            return carry

        lax.fori_loop(0, DEVICES // 8, unpack, 0)

    def analyse_y(source):
        def step(index, carry):
            pair = (index // GROUPS) * 2
            group = index % GROUPS
            channels = pl.ds(group * GROUP, GROUP)
            planes = [
                source[channels, pair + inner].reshape(GROUP * NY, NZ) for inner in range(2)
            ]
            first = matmul(analysis_y[...], jnp.concatenate(planes, 1))
            first = first.reshape(2, MY, GROUP, 2 * NZ)
            for inner in range(2):
                row = pl.multiple_of((pair + inner) * C + group * GROUP, GROUP)
                for part in range(2):
                    grid[:, pl.ds(row, GROUP), part * NZ:(part + 1) * NZ] = first[
                        part, :, :, inner * NZ:(inner + 1) * NZ
                    ]
            return carry

        lax.fori_loop(0, 2 * GROUPS, step, 0)

    def analyse_z(turn):
        def step(index, carry):
            ky = (me // HIGH + index) % MY
            first = grid[ky].astype(BF16)
            second = lax.dot_general(
                analysis_z[...], first, (((1,), (1,)), ((), ())), preferred_element_type=F32
            )
            for high in range(HIGH):
                target = ky * HIGH + high
                sent[turn, target] = second[4 * high:4 * high + 4].astype(BF16)
                send(turn, target)
            return carry

        lax.fori_loop(0, MY, step, 0)

    def analyse_x(target, scale):
        for sample in range(BATCHES):
            parts = []
            for row in range(2 * HELD):
                block = flat[pl.ds(sample * 4 + row, SLABS, stride=DEVICES // SLABS * 4), :]
                stacked = jnp.concatenate(lane_groups(block), 0).astype(BF16)
                parts.append(matmul(analysis_x[...], stacked))
            real = [parts[b][:MX] + parts[HELD + b][MX:] for b in range(HELD)]
            imag = [parts[HELD + b][:MX] - parts[b][MX:] for b in range(HELD)]
            turned = jnp.concatenate(real + imag, 0).T
            total = turned[:C] + turned[C:2 * C] + turned[2 * C:3 * C] + turned[3 * C:]
            target[sample] = total * scale

    def synthesise_x(turn):
        half = HELD * MX
        for sample in range(BATCHES):
            rounded = modes[sample].astype(BF16).astype(F32)
            turned = jnp.concatenate([rounded] * WIDTH, 0).T
            for part in range(2):
                for b in range(HELD):
                    real = turned[b * MX:(b + 1) * MX]
                    imag = turned[half + b * MX:half + (b + 1) * MX]
                    pair = [real, -imag] if part == 0 else [imag, real]
                    stacked = jnp.concatenate(
                        lane_groups(jnp.concatenate(pair, 0)), 0
                    ).astype(BF16)
                    flat[pl.ds(sample * 4 + part * HELD + b, SLABS, stride=DEVICES // SLABS * 4), :] = (
                        matmul(synthesis_x[...], stacked)
                    )

        def step(index, carry):
            slab = (me // BATCHES + index) % SLABS
            for sample in range(BATCHES):
                target = slab * BATCHES + sample
                sent[turn, target] = flat[
                    pl.ds(pl.multiple_of(target * 4, 4), 4), :
                ].astype(BF16)
                send(turn, target)
            return carry

        lax.fori_loop(0, SLABS, step, 0)

    def synthesise_z():
        def step(ky, carry):
            block = flat[pl.ds(pl.multiple_of(ky * 2 * MZ, 2 * MZ), 2 * MZ), :].T.astype(BF16)
            grid[ky] = matmul(block, synthesis_z[...])
            return carry

        lax.fori_loop(0, MY, step, 0)

    def synthesise_y(finish):
        def step(index, carry):
            pair = (index // GROUPS) * 2
            group = index % GROUPS
            columns = []
            for inner in range(2):
                row = pl.multiple_of((pair + inner) * C + group * GROUP, GROUP)
                halves = [
                    grid[:, pl.ds(row, GROUP), part * NZ:(part + 1) * NZ].reshape(MY * GROUP, NZ)
                    for part in range(2)
                ]
                columns.append(jnp.concatenate(halves, 0).astype(BF16))
            result[...] = matmul(synthesis_y[...], jnp.concatenate(columns, 1))

            def one(channel, carry):
                rows = pl.ds(pl.multiple_of(channel * NY, NY), NY)
                for inner in range(2):
                    finish(
                        group * GROUP + channel,
                        pair + inner,
                        result[rows, inner * NZ:(inner + 1) * NZ],
                    )
                return carry

            lax.fori_loop(0, GROUP, one, 0)
            return carry

        lax.fori_loop(0, 2 * GROUPS, step, 0)

    def pointwise(source, weight):
        spread_map[...] = spread(weight)

        def step(index, carry):
            pair = (index // (NY // BAND)) * 2
            band = pl.ds(pl.multiple_of((index % (NY // BAND)) * BAND, BAND), BAND)
            columns = [source[:, pair + inner, band, :].reshape(C * BAND, NZ) for inner in range(2)]
            product = matmul(spread_map[...], jnp.concatenate(columns, 1))
            for inner in range(2):
                linear[:, pair + inner, band, :] = product[
                    :, inner * NZ:(inner + 1) * NZ
                ].reshape(C, BAND, NZ)
            return carry

        lax.fori_loop(0, 2 * (NY // BAND), step, 0)

    def double_weights(channel, carry):
        for part in range(2):
            block = weights[part, channel].astype(F32)
            doubled[part, channel] = jnp.concatenate([block, block], 1)
        return carry

    lower = lax.broadcasted_iota(jnp.int32, (C, 2 * HELD * MX), 1) < HELD * MX

    def swapped(block):
        return pltpu.roll(block, HELD * MX, 1)

    def mix():
        for sample in range(BATCHES):
            turned = swapped(values[sample])
            grads[sample] = jnp.where(lower, -turned, turned)

        def step(channel, totals):
            real, imag = doubled[0, channel], doubled[1, channel]
            return tuple(
                totals[sample]
                + real * values[sample, pl.ds(channel, 1), :]
                + imag * grads[sample, pl.ds(channel, 1), :]
                for sample in range(BATCHES)
            )

        start = tuple(jnp.zeros((C, 2 * HELD * MX), F32) for _ in range(BATCHES))
        totals = lax.fori_loop(0, C, step, start)
        for sample in range(BATCHES):
            modes[sample] = totals[sample]

    def turned_grads(sample):
        turned = swapped(grads[sample])
        return jnp.where(lower, turned, -turned)

    def back_mix():
        for sample in range(BATCHES):
            straight, other = grads[sample], turned_grads(sample)

            def step(channel, carry):
                product = doubled[0, channel] * straight + doubled[1, channel] * other
                modes[sample, pl.ds(channel, 1), :] = jnp.sum(product, 0, keepdims=True)
                return carry

            lax.fori_loop(0, C, step, 0)

    def weight_products():
        for sample in range(BATCHES):
            turned = swapped(values[sample])
            modes[sample] = jnp.where(lower, values[sample], turned)
            values[sample] = jnp.where(lower, turned, values[sample])
        straight = [grads[sample] for sample in range(BATCHES)]
        other = [turned_grads(sample) for sample in range(BATCHES)]

        def step(channel, carry):
            total = jnp.zeros((C, 2 * HELD * MX), F32)
            for sample in range(BATCHES):
                total = total + straight[sample] * modes[sample, pl.ds(channel, 1), :]
                total = total + other[sample] * values[sample, pl.ds(channel, 1), :]
            weight_grad[0, channel] = total[:, :HELD * MX]
            weight_grad[1, channel] = total[:, HELD * MX:]
            return carry

        lax.fori_loop(0, C, step, 0)

    analyse_y(fields)
    pl.semaphore_wait(barrier, DEVICES - 1)
    analyse_z(0)
    pointwise(fields, forward_map[...])
    lax.fori_loop(0, C, double_weights, 0)
    receive(0)
    analyse_x(values, SCALE_IN)
    mix()
    synthesise_x(1)
    receive(1)
    synthesise_z()

    def forward_finish(channel, x, part):
        slopes = gelu_slope(linear[channel, x] + part * SCALE_OUT)
        slope[channel, x] = (cotangent[channel, x].astype(F32) * slopes).astype(BF16)

    synthesise_y(forward_finish)
    analyse_y(slope)
    analyse_z(2)
    pointwise(slope, backward_map[...])
    receive(2)
    analyse_x(grads, SCALE_OUT)
    back_mix()
    synthesise_x(3)
    weight_products()
    receive(3)
    synthesise_z()

    def backward_finish(channel, x, part):
        field_grad[channel, x] = (linear[channel, x] + part * SCALE_IN).astype(BF16)

    synthesise_y(backward_finish)
    some = pl.ds(0, DEVICES - 1)
    for turn in range(4):
        pltpu.make_async_copy(
            sent.at[turn, some], got.at[turn, some], send_sem.at[turn]
        ).wait()


def body(fields, cotangent, local_weight, spectral_weight):
    shape = (C, WIDTH, NY, NZ)
    lanes = 2 * HELD * MX
    operands = (
        fields.reshape(shape), cotangent.reshape(shape), local_weight.T, local_weight,
        spectral_weight, *make_tables(),
    )
    field_grad, weight_grad = pl.pallas_call(
        kernel,
        out_shape=(
            jax.ShapeDtypeStruct(shape, BF16),
            jax.ShapeDtypeStruct((2, C, C, HELD * MX), F32),
        ),
        in_specs=[pl.BlockSpec(memory_space=pltpu.VMEM)] * len(operands),
        out_specs=[pl.BlockSpec(memory_space=pltpu.VMEM)] * 2,
        scratch_shapes=[
            pltpu.VMEM((4, DEVICES, 4, 128), BF16),
            pltpu.VMEM((4, DEVICES, 4, 128), BF16),
            pltpu.VMEM((MY, WIDTH * C, 2 * NZ), F32),
            pltpu.VMEM((DEVICES * 4, 128), F32),
            pltpu.VMEM(shape, F32),
            pltpu.VMEM(shape, BF16),
            pltpu.VMEM((2, C, C, lanes), F32),
            pltpu.VMEM((BATCHES, C, lanes), F32),
            pltpu.VMEM((BATCHES, C, lanes), F32),
            pltpu.VMEM((BATCHES, C, lanes), F32),
            pltpu.VMEM((GROUP * NY, 2 * NZ), F32),
            pltpu.VMEM((C * BAND, C * BAND), BF16),
            pltpu.SemaphoreType.DMA((4,)),
            pltpu.SemaphoreType.DMA((4,)),
            pltpu.SemaphoreType.DMA((4,)),
        ],
        compiler_params=pltpu.CompilerParams(
            collective_id=0, has_side_effects=True, vmem_limit_bytes=60 << 20
        ),
    )(*operands)
    return (field_grad.reshape(fields.shape), weight_grad)


def solution(mesh):
    placed = (
        P("batch", None, "slab", None, None),
        P("batch", None, "slab", None, None),
        P(),
        P(None, None, None, ("slab", "batch")),
    )
    return jax.shard_map(
        body,
        mesh=mesh,
        in_specs=placed,
        out_specs=(P("batch", None, "slab", None, None), P(None, None, None, ("slab", "batch"))),
        check_vma=False,
    )
```

```python
from functools import partial
import math

import jax
import jax.numpy as jnp
import ml_dtypes
import numpy as np
from jax import lax
from jax.experimental import pallas as pl
from jax.experimental.pallas import tpu as pltpu
from jax.sharding import PartitionSpec as P

C = 32
NX = 256
NY = 128
NZ = 128
MX = 32
MY = 32
MZ = 16
SLABS = 64
BATCHES = 4
DEVICES = SLABS * BATCHES
WIDTH = NX // SLABS
HELD = MY * MZ // DEVICES
HIGH = MZ // HELD
GROUP = 8
GROUPS = C // GROUP
BAND = 16
SOME_KY = 4
MESH = pl.DeviceIdType.MESH
F32 = jnp.float32
BF16 = jnp.bfloat16
SCALE_IN = 1.0 / math.sqrt(NX * NY * NZ)
SCALE_OUT = 1.0 / math.sqrt(MX * MY * MZ * C)


def wave_table(number, length, signed):
    numbers = np.arange(number)
    if signed:
        numbers = np.where(numbers < number // 2, numbers, numbers - number)
    phases = np.mod(numbers[:, None] * np.arange(length)[None, :], length).astype(np.float32)
    angles = phases * np.float32(2.0 * math.pi / length)
    return (np.cos(angles).astype(np.float32), np.sin(angles).astype(np.float32))


def make_tables():
    cos_y, sin_y = wave_table(MY, NY, True)
    cos_z, sin_z = wave_table(MZ, NZ, False)
    cos_x, sin_x = wave_table(MX, NX, True)
    eye = np.eye(GROUP, dtype=np.float32)
    pair_y = np.stack([cos_y, -sin_y])
    analysis_y = np.einsum("pky,ab->pkaby", pair_y, eye).reshape(2 * MY * GROUP, GROUP * NY)
    synthesis_y = np.einsum("pky,ab->aypkb", pair_y, eye).reshape(GROUP * NY, 2 * MY * GROUP)
    analysis_z = np.stack([np.stack([cos_z, sin_z], 1), np.stack([-sin_z, cos_z], 1)])
    analysis_z = analysis_z.reshape(2, HIGH, HELD, 2 * NZ).transpose(1, 0, 2, 3).reshape(2 * MZ, 2 * NZ)
    synthesis_z = np.stack([np.stack([cos_z, sin_z], 1), np.stack([-sin_z, cos_z], 1)])
    synthesis_z = synthesis_z.reshape(2, HIGH, HELD, 2 * NZ).transpose(1, 0, 2, 3).reshape(2 * MZ, 2 * NZ)
    synthesis_z = np.kron(np.eye(SOME_KY, dtype=np.float32), synthesis_z)
    both_x = np.stack([cos_x, sin_x]).reshape(2, MX, SLABS, WIDTH).transpose(0, 1, 3, 2)
    analysis_x = both_x.reshape(2 * MX, WIDTH * SLABS)
    synthesis_x = both_x.transpose(3, 2, 0, 1).reshape(SLABS, WIDTH * 2 * MX)
    tables = (analysis_y, synthesis_y, analysis_z, synthesis_z, analysis_x, synthesis_x)
    return tuple(np.ascontiguousarray(table).astype(ml_dtypes.bfloat16) for table in tables)


def matmul(left, right):
    return jnp.dot(left, right, preferred_element_type=F32)


def gelu_slope(values):
    size = jnp.abs(values)
    inverse = 1.0 / (1.0 + (0.3275911 / math.sqrt(2.0)) * size)
    tail = 0.5 * 1.061405429 * inverse - 0.5 * 1.453152027
    tail = tail * inverse + 0.5 * 1.421413741
    tail = tail * inverse - 0.5 * 0.284496736
    tail = tail * inverse + 0.5 * 0.254829592
    tail = tail * inverse - size * (1.0 / math.sqrt(2.0 * math.pi))
    below = jnp.exp(-0.5 * values * values) * tail
    return jnp.where(values >= 0.0, 1.0 - below, below)


def lane_groups(value):
    lanes = lax.broadcasted_iota(jnp.int32, value.shape, 1) // C
    return [jnp.where(lanes == group, value, 0.0) for group in range(WIDTH)]


def spread(weight, turned):
    rows = C * BAND
    left = (
        lax.broadcasted_iota(jnp.int32, (rows, C), 0) // BAND
        == lax.broadcasted_iota(jnp.int32, (rows, C), 1)
    ).astype(F32).astype(BF16)
    right = (
        lax.broadcasted_iota(jnp.int32, (C, rows), 1) // BAND
        == lax.broadcasted_iota(jnp.int32, (C, rows), 0)
    ).astype(F32).astype(BF16)
    side = 1 if turned else 0
    tall = lax.dot_general(left, weight, (((1,), (side,)), ((), ())), preferred_element_type=F32)
    whole = matmul(tall.astype(BF16), right)
    same = (
        lax.broadcasted_iota(jnp.int32, (rows, rows), 0) % BAND
        == lax.broadcasted_iota(jnp.int32, (rows, rows), 1) % BAND
    )
    return jnp.where(same, whole, 0.0).astype(BF16)


def unpack(source, flat):
    def step(index, carry):
        for inner in range(8):
            tile = index * 8 + inner
            flat[pl.ds(pl.multiple_of(tile * 4, 4), 4), :] = source[tile].astype(F32)
        return carry

    lax.fori_loop(0, DEVICES // 8, step, 0)


def synthesise_z(flat, grid, table):
    rows = SOME_KY * 2 * MZ

    def step(index, carry):
        block = flat[pl.ds(pl.multiple_of(index * rows, rows), rows), :].T.astype(BF16)
        second = matmul(block, table[...])
        for inner in range(SOME_KY):
            grid[index * SOME_KY + inner] = second[:, inner * 2 * NZ:(inner + 1) * 2 * NZ]
        return carry

    lax.fori_loop(0, MY // SOME_KY, step, 0)


def synthesise_y(grid, table, result, finish):
    def step(index, carry):
        pair = (index // GROUPS) * 2
        group = index % GROUPS
        columns = []
        for inner in range(2):
            row = pl.multiple_of((pair + inner) * C + group * GROUP, GROUP)
            halves = [
                grid[:, pl.ds(row, GROUP), part * NZ:(part + 1) * NZ].reshape(MY * GROUP, NZ)
                for part in range(2)
            ]
            columns.append(jnp.concatenate(halves, 0).astype(BF16))
        result[...] = matmul(table[...], jnp.concatenate(columns, 1))
        finish(group * GROUP, pair, index)
        return carry

    lax.fori_loop(0, 2 * GROUPS, step, 0)


def each_plane(result, apply):
    def one(channel, carry):
        rows = pl.ds(pl.multiple_of(channel * NY, NY), NY)
        for inner in range(2):
            apply(channel, inner, result[rows, inner * NZ:(inner + 1) * NZ])
        return carry

    lax.fori_loop(0, GROUP, one, 0)


def kernel(
    fields_hbm, cotangent_hbm, weights_hbm, analysis_y_hbm, synthesis_y_hbm, synthesis_z_hbm,
    local_weight, analysis_z, analysis_x, synthesis_x,
    through_hbm, last, weight_part,
    fields, cotangent, weights, analysis_y, synthesis_y, synthesis_z,
    sent, got, grid, flat, linear, slope, through, doubled, values, grads, modes, result,
    spread_map, send_sem, recv_sem, own_sem, load_sem, store_sem,
):
    me = lax.axis_index("slab") * BATCHES + lax.axis_index("batch")

    def place(index):
        return (index // BATCHES, index % BATCHES)

    loads = [
        pltpu.make_async_copy(source, target, load_sem.at[index])
        for index, (source, target) in enumerate((
            (analysis_y_hbm, analysis_y), (fields_hbm, fields), (weights_hbm, weights),
            (synthesis_z_hbm, synthesis_z), (synthesis_y_hbm, synthesis_y),
            (cotangent_hbm, cotangent),
        ))
    ]
    for load in loads:
        load.start()
    barrier = pltpu.get_barrier_semaphore()

    def greet(step, carry):
        pl.semaphore_signal(
            barrier, inc=1, device_id=place((me + step) % DEVICES), device_id_type=MESH
        )
        return carry

    lax.fori_loop(1, DEVICES, greet, 0)

    def send(turn, target):
        @pl.when(target != me)
        def _():
            pltpu.make_async_remote_copy(
                src_ref=sent.at[turn, target],
                dst_ref=got.at[turn, me],
                send_sem=send_sem.at[turn],
                recv_sem=recv_sem.at[turn],
                device_id=place(target),
                device_id_type=MESH,
            ).start()

        @pl.when(target == me)
        def _():
            pltpu.make_async_copy(
                sent.at[turn, me], got.at[turn, me], own_sem.at[turn]
            ).start()

    def wait_messages(turn):
        pltpu.make_async_copy(sent.at[turn, me], got.at[turn, me], own_sem.at[turn]).wait()
        some = pl.ds(0, DEVICES - 1)
        pltpu.make_async_copy(
            sent.at[turn, some], got.at[turn, some], recv_sem.at[turn]
        ).wait()


    def receive(turn):
        wait_messages(turn)
        unpack(got.at[turn], flat)

    def analyse_y(source):
        def step(index, carry):
            pair = (index // GROUPS) * 2
            group = index % GROUPS
            channels = pl.ds(group * GROUP, GROUP)
            planes = [
                source[channels, pair + inner].reshape(GROUP * NY, NZ) for inner in range(2)
            ]
            first = matmul(analysis_y[...], jnp.concatenate(planes, 1))
            first = first.reshape(2, MY, GROUP, 2 * NZ)
            for inner in range(2):
                row = pl.multiple_of((pair + inner) * C + group * GROUP, GROUP)
                for part in range(2):
                    grid[:, pl.ds(row, GROUP), part * NZ:(part + 1) * NZ] = first[
                        part, :, :, inner * NZ:(inner + 1) * NZ
                    ]
            return carry

        lax.fori_loop(0, 2 * GROUPS, step, 0)

    def analyse_z(turn):
        def step(index, carry):
            batch = [(me // HIGH + index * SOME_KY + inner) % MY for inner in range(SOME_KY)]
            seconds = [
                lax.dot_general(
                    analysis_z[...], grid[ky].astype(BF16), (((1,), (1,)), ((), ())),
                    preferred_element_type=F32,
                )
                for ky in batch
            ]
            for ky, second in zip(batch, seconds):
                for high in range(HIGH):
                    sent[turn, ky * HIGH + high] = second[4 * high:4 * high + 4].astype(BF16)

            def start(high, carry):
                for ky in batch:
                    send(turn, ky * HIGH + high)
                return carry

            lax.fori_loop(0, HIGH, start, 0)
            return carry

        lax.fori_loop(0, MY // SOME_KY, step, 0)

    def analyse_x(target, scale):
        for sample in range(BATCHES):
            parts = []
            for row in range(2 * HELD):
                block = flat[pl.ds(sample * 4 + row, SLABS, stride=DEVICES // SLABS * 4), :]
                stacked = jnp.concatenate(lane_groups(block), 0).astype(BF16)
                parts.append(matmul(analysis_x[...], stacked))
            real = [parts[b][:MX] + parts[HELD + b][MX:] for b in range(HELD)]
            imag = [parts[HELD + b][:MX] - parts[b][MX:] for b in range(HELD)]
            turned = jnp.concatenate(real + imag, 0).T
            total = turned[:C] + turned[C:2 * C] + turned[2 * C:3 * C] + turned[3 * C:]
            target[sample] = total * scale

    def synthesise_x(turn):
        half = HELD * MX
        for sample in range(BATCHES):
            rounded = modes[sample].astype(BF16).astype(F32)
            turned = jnp.concatenate([rounded] * WIDTH, 0).T
            for part in range(2):
                for b in range(HELD):
                    real = turned[b * MX:(b + 1) * MX]
                    imag = turned[half + b * MX:half + (b + 1) * MX]
                    pair = [real, -imag] if part == 0 else [imag, real]
                    stacked = jnp.concatenate(
                        lane_groups(jnp.concatenate(pair, 0)), 0
                    ).astype(BF16)
                    flat[pl.ds(sample * 4 + part * HELD + b, SLABS, stride=DEVICES // SLABS * 4), :] = (
                        matmul(synthesis_x[...], stacked)
                    )

        def step(index, carry):
            slab = (me // BATCHES + index) % SLABS
            for sample in range(BATCHES):
                target = slab * BATCHES + sample
                sent[turn, target] = flat[
                    pl.ds(pl.multiple_of(target * 4, 4), 4), :
                ].astype(BF16)
                send(turn, target)
            return carry

        lax.fori_loop(0, SLABS, step, 0)

    def pointwise(source, turned, target):
        spread_map[...] = spread(local_weight[...], turned)

        def step(index, carry):
            pair = (index // (NY // BAND)) * 2
            band = pl.ds(pl.multiple_of((index % (NY // BAND)) * BAND, BAND), BAND)
            columns = [source[:, pair + inner, band, :].reshape(C * BAND, NZ) for inner in range(2)]
            product = matmul(spread_map[...], jnp.concatenate(columns, 1))
            for inner in range(2):
                target[:, pair + inner, band, :] = product[
                    :, inner * NZ:(inner + 1) * NZ
                ].reshape(C, BAND, NZ).astype(target.dtype)
            return carry

        lax.fori_loop(0, 2 * (NY // BAND), step, 0)

    def double_weights(channel, carry):
        for part in range(2):
            block = weights[part, channel].astype(F32)
            doubled[part, channel] = jnp.concatenate([block, block], 1)
        return carry

    lower = lax.broadcasted_iota(jnp.int32, (C, 2 * HELD * MX), 1) < HELD * MX

    def swapped(block):
        return pltpu.roll(block, HELD * MX, 1)

    def mix():
        for sample in range(BATCHES):
            turned = swapped(values[sample])
            grads[sample] = jnp.where(lower, -turned, turned)

        def step(channel, totals):
            real, imag = doubled[0, channel], doubled[1, channel]
            return tuple(
                totals[sample]
                + real * values[sample, pl.ds(channel, 1), :]
                + imag * grads[sample, pl.ds(channel, 1), :]
                for sample in range(BATCHES)
            )

        start = tuple(jnp.zeros((C, 2 * HELD * MX), F32) for _ in range(BATCHES))
        totals = lax.fori_loop(0, C, step, start)
        for sample in range(BATCHES):
            modes[sample] = totals[sample]

    def turned_grads(sample):
        turned = swapped(grads[sample])
        return jnp.where(lower, turned, -turned)

    def back_mix():
        for sample in range(BATCHES):
            straight, other = grads[sample], turned_grads(sample)

            def step(channel, carry):
                product = doubled[0, channel] * straight + doubled[1, channel] * other
                modes[sample, pl.ds(channel, 1), :] = jnp.sum(product, 0, keepdims=True)
                return carry

            lax.fori_loop(0, C, step, 0)

    def weight_products():
        for sample in range(BATCHES):
            turned = swapped(values[sample])
            modes[sample] = jnp.where(lower, values[sample], turned)
            values[sample] = jnp.where(lower, turned, values[sample])
        straight = [grads[sample] for sample in range(BATCHES)]
        other = [turned_grads(sample) for sample in range(BATCHES)]

        def step(channel, carry):
            total = jnp.zeros((C, 2 * HELD * MX), F32)
            for sample in range(BATCHES):
                total = total + straight[sample] * modes[sample, pl.ds(channel, 1), :]
                total = total + other[sample] * values[sample, pl.ds(channel, 1), :]
            weight_part[channel] = total
            return carry

        lax.fori_loop(0, C, step, 0)

    def forward_finish(channel, x, index):
        def apply(offset, inner, part):
            place = (channel + offset, x + inner)
            slopes = gelu_slope(linear[place] + part * SCALE_OUT)
            slope[place] = (cotangent[place].astype(F32) * slopes).astype(BF16)

        each_plane(result, apply)

    loads[0].wait()
    loads[1].wait()
    analyse_y(fields)
    pl.semaphore_wait(barrier, DEVICES - 1)
    analyse_z(0)
    pointwise(fields, True, linear)
    for load in loads[2:]:
        load.wait()
    lax.fori_loop(0, C, double_weights, 0)
    receive(0)
    analyse_x(values, SCALE_IN)
    mix()
    synthesise_x(1)
    receive(1)
    synthesise_z(flat, grid, synthesis_z)
    synthesise_y(grid, synthesis_y, result, forward_finish)
    analyse_y(slope)
    analyse_z(2)
    pointwise(slope, False, through)
    store = pltpu.make_async_copy(through, through_hbm, store_sem)
    store.start()
    receive(2)
    analyse_x(grads, SCALE_OUT)
    back_mix()
    synthesise_x(3)
    weight_products()
    store.wait()
    wait_messages(3)
    last[...] = got[3]
    some = pl.ds(0, DEVICES - 1)
    for turn in range(4):
        pltpu.make_async_copy(
            sent.at[turn, some], got.at[turn, some], send_sem.at[turn]
        ).wait()


def last_kernel(
    messages, synthesis_z, synthesis_y, through_hbm, field_grad_hbm,
    grid, flat, result, through, field_grad, load_sem, store_sem,
):

    def some(index):
        return (pl.ds((index % GROUPS) * GROUP, GROUP), pl.ds((index // GROUPS) * 2, 2))

    def load(index):
        return pltpu.make_async_copy(
            through_hbm.at[some(index)], through.at[some(index)], load_sem.at[index]
        )

    def store(index):
        return pltpu.make_async_copy(
            field_grad.at[some(index)], field_grad_hbm.at[some(index)], store_sem.at[index]
        )

    for index in range(2 * GROUPS):
        load(index).start()
    unpack(messages, flat)
    synthesise_z(flat, grid, synthesis_z)

    def finish(channel, x, index):
        load(index).wait()

        def apply(offset, inner, part):
            place = (channel + offset, x + inner)
            field_grad[place] = (through[place].astype(F32) + part * SCALE_IN).astype(BF16)

        each_plane(result, apply)
        store(index).start()

    synthesise_y(grid, synthesis_y, result, finish)
    for index in range(2 * GROUPS):
        store(index).wait()


def body(fields, cotangent, local_weight, spectral_weight):
    shape = (C, WIDTH, NY, NZ)
    lanes = 2 * HELD * MX
    analysis_y, synthesis_y, analysis_z, synthesis_z, analysis_x, synthesis_x = make_tables()
    far = (
        fields.reshape(shape), cotangent.reshape(shape), spectral_weight,
        analysis_y, synthesis_y, synthesis_z,
    )
    near = (local_weight, analysis_z, analysis_x, synthesis_x)
    in_vmem, anywhere = pl.BlockSpec(memory_space=pltpu.VMEM), pl.BlockSpec(memory_space=pl.ANY)
    field_shape = jax.ShapeDtypeStruct(shape, BF16)
    message_shape = jax.ShapeDtypeStruct((DEVICES, 4, 128), BF16)
    part_shape = jax.ShapeDtypeStruct((C, C, lanes), F32)
    through, messages, part = pl.pallas_call(
        kernel,
        out_shape=(field_shape, message_shape, part_shape),
        in_specs=[anywhere] * len(far) + [in_vmem] * len(near),
        out_specs=[anywhere, in_vmem, in_vmem],
        scratch_shapes=[pltpu.VMEM(array.shape, BF16) for array in far] + [
            pltpu.VMEM((4, DEVICES, 4, 128), BF16),
            pltpu.VMEM((4, DEVICES, 4, 128), BF16),
            pltpu.VMEM((MY, WIDTH * C, 2 * NZ), F32),
            pltpu.VMEM((DEVICES * 4, 128), F32),
            pltpu.VMEM(shape, F32),
            pltpu.VMEM(shape, BF16),
            pltpu.VMEM(shape, BF16),
            pltpu.VMEM((2, C, C, lanes), F32),
            pltpu.VMEM((BATCHES, C, lanes), F32),
            pltpu.VMEM((BATCHES, C, lanes), F32),
            pltpu.VMEM((BATCHES, C, lanes), F32),
            pltpu.VMEM((GROUP * NY, 2 * NZ), F32),
            pltpu.VMEM((C * BAND, C * BAND), BF16),
            pltpu.SemaphoreType.DMA((4,)),
            pltpu.SemaphoreType.DMA((4,)),
            pltpu.SemaphoreType.DMA((4,)),
            pltpu.SemaphoreType.DMA((len(far),)),
            pltpu.SemaphoreType.DMA,
        ],
        compiler_params=pltpu.CompilerParams(
            collective_id=0, has_side_effects=True, vmem_limit_bytes=60 << 20
        ),
    )(*far, *near)
    field_grad = pl.pallas_call(
        last_kernel,
        out_shape=field_shape,
        in_specs=[in_vmem] * 3 + [anywhere],
        out_specs=anywhere,
        scratch_shapes=[
            pltpu.VMEM((MY, WIDTH * C, 2 * NZ), F32),
            pltpu.VMEM((DEVICES * 4, 128), F32),
            pltpu.VMEM((GROUP * NY, 2 * NZ), F32),
            pltpu.VMEM(shape, BF16),
            pltpu.VMEM(shape, BF16),
            pltpu.SemaphoreType.DMA((2 * GROUPS,)),
            pltpu.SemaphoreType.DMA((2 * GROUPS,)),
        ],
        compiler_params=pltpu.CompilerParams(vmem_limit_bytes=60 << 20),
    )(messages, synthesis_z, synthesis_y, through)
    weight_grad = jnp.stack([part[:, :, :HELD * MX], part[:, :, HELD * MX:]], 0)
    return (field_grad.reshape(fields.shape), weight_grad)


def solution(mesh):
    placed = (
        P("batch", None, "slab", None, None),
        P("batch", None, "slab", None, None),
        P(),
        P(None, None, None, ("slab", "batch")),
    )
    return jax.shard_map(
        body,
        mesh=mesh,
        in_specs=placed,
        out_specs=(P("batch", None, "slab", None, None), P(None, None, None, ("slab", "batch"))),
        check_vma=False,
    )
```

```python
import math

import jax
import jax.numpy as jnp
import ml_dtypes
import numpy as np
from jax import lax
from jax.experimental import pallas as pl
from jax.experimental.pallas import tpu as pltpu
from jax.sharding import PartitionSpec as P

C = 32
NX = 256
NY = 128
NZ = 128
MX = 32
MY = 32
MZ = 16
SLABS = 64
BATCHES = 4
WIDTH = NX // SLABS
HELD = 2
HIGH = MZ // HELD
MODES = HELD * MX
LANES = 2 * MODES
ROWS = 2 * BATCHES
GROUP = 8
GROUPS = C // GROUP
BAND = 16
SOME_KY = 8
MESH = pl.DeviceIdType.MESH
F32 = jnp.float32
BF16 = jnp.bfloat16
SCALE_IN = 1.0 / math.sqrt(NX * NY * NZ)
SCALE_OUT = 1.0 / math.sqrt(MX * MY * MZ * C)


def wave_table(number, length, signed):
    numbers = np.arange(number)
    if signed:
        numbers = np.where(numbers < number // 2, numbers, numbers - number)
    phases = np.mod(numbers[:, None] * np.arange(length)[None, :], length).astype(np.float32)
    angles = phases * np.float32(2.0 * math.pi / length)
    return (np.cos(angles).astype(np.float32), np.sin(angles).astype(np.float32))


def make_tables():
    cos_y, sin_y = wave_table(MY, NY, True)
    cos_z, sin_z = wave_table(MZ, NZ, False)
    cos_x, sin_x = wave_table(MX, NX, True)
    eye = np.eye(GROUP, dtype=np.float32)
    pair_y = np.stack([cos_y, -sin_y])
    analysis_y = np.einsum("pky,ab->pkaby", pair_y, eye).reshape(2 * MY * GROUP, GROUP * NY)
    synthesis_y = np.einsum("pky,ab->aypkb", pair_y, eye).reshape(GROUP * NY, 2 * MY * GROUP)
    both_z = np.stack([np.stack([cos_z, sin_z], 1), np.stack([-sin_z, cos_z], 1)])
    both_z = both_z.reshape(2, HIGH, HELD, 2 * NZ)
    analysis_z = both_z.transpose(2, 1, 0, 3).reshape(2 * MZ, 2 * NZ)
    several = np.eye(SOME_KY, dtype=np.float32)
    synthesis_z = np.einsum("qhlw,ab->lahqbw", both_z, several)
    synthesis_z = synthesis_z.reshape(SOME_KY * 2 * MZ, SOME_KY * 2 * NZ)
    both_x = np.stack([cos_x, sin_x]).reshape(2, MX, SLABS, WIDTH).transpose(0, 1, 3, 2)
    analysis_x = both_x.reshape(2 * MX, WIDTH * SLABS)
    synthesis_x = both_x.reshape(2, MX, 2, 2, SLABS).transpose(2, 4, 3, 0, 1)
    synthesis_x = synthesis_x.reshape(2 * SLABS, 2 * 2 * MX)
    tables = (analysis_y, synthesis_y, analysis_z, synthesis_z, analysis_x, synthesis_x)
    return tuple(np.ascontiguousarray(table).astype(ml_dtypes.bfloat16) for table in tables)


def matmul(left, right):
    return jnp.dot(left, right, preferred_element_type=F32)


def gelu_slope(values):
    size = jnp.abs(values)
    below = 1.0 + (0.3275911 / math.sqrt(2.0)) * size
    inverse = pl.reciprocal(below, approx=True)
    inverse = inverse * (2.0 - below * inverse)
    tail = 0.5 * 1.061405429 * inverse - 0.5 * 1.453152027
    tail = tail * inverse + 0.5 * 1.421413741
    tail = tail * inverse - 0.5 * 0.284496736
    tail = tail * inverse + 0.5 * 0.254829592
    tail = tail * inverse - size * (1.0 / math.sqrt(2.0 * math.pi))
    below = jnp.exp2((-0.5 / math.log(2.0)) * (values * values)) * tail
    return jnp.where(values >= 0.0, 1.0 - below, below)


def lane_index(shape):
    return lax.broadcasted_iota(jnp.int32, shape, len(shape) - 1)


def split_cells(value):
    second = (lane_index(value.shape) // C) % 2 == 1
    return [jnp.where(second, 0.0, value), jnp.where(second, value, 0.0)]


def spread(weight, turned):
    rows = C * BAND
    left = (
        lax.broadcasted_iota(jnp.int32, (rows, C), 0) // BAND
        == lax.broadcasted_iota(jnp.int32, (rows, C), 1)
    ).astype(F32).astype(BF16)
    right = (
        lax.broadcasted_iota(jnp.int32, (C, rows), 1) // BAND
        == lax.broadcasted_iota(jnp.int32, (C, rows), 0)
    ).astype(F32).astype(BF16)
    side = 1 if turned else 0
    tall = lax.dot_general(left, weight, (((1,), (side,)), ((), ())), preferred_element_type=F32)
    whole = matmul(tall.astype(BF16), right)
    same = (
        lax.broadcasted_iota(jnp.int32, (rows, rows), 0) % BAND
        == lax.broadcasted_iota(jnp.int32, (rows, rows), 1) % BAND
    )
    return jnp.where(same, whole, 0.0).astype(BF16)


def unpack(source, flat):
    def step(index, carry):
        for inner in range(8):
            tile = index * 8 + inner
            flat[pl.ds(pl.multiple_of(tile * ROWS, ROWS), ROWS), :] = source[tile].astype(F32)
        return carry

    lax.fori_loop(0, SLABS // 8, step, 0)


def synthesise_z(flat, grid, table):
    rows = SOME_KY * MZ
    half = LANES // 2
    batches = MY // SOME_KY
    blocks = []
    for batch in range(batches):
        turned = flat[pl.ds(batch * rows, rows), :].T
        blocks.append(jnp.concatenate([turned[:half], turned[half:]], 1))
    left = jnp.concatenate(blocks, 0).astype(BF16)
    for inner in range(SOME_KY):
        second = matmul(left, table[:, inner * 2 * NZ:(inner + 1) * 2 * NZ])
        for batch in range(batches):
            grid[batch * SOME_KY + inner] = second[batch * half:(batch + 1) * half]


def synthesise_y(grid, table, result, finish):
    def step(group, carry):
        columns = []
        for inner in range(2):
            row = pl.multiple_of(inner * C + group * GROUP, GROUP)
            halves = [
                grid[:, pl.ds(row, GROUP), part * NZ:(part + 1) * NZ].reshape(MY * GROUP, NZ)
                for part in range(2)
            ]
            columns.append(jnp.concatenate(halves, 0).astype(BF16))
        result[...] = matmul(table[...], jnp.concatenate(columns, 1))
        finish(group)
        return carry

    lax.fori_loop(0, GROUPS, step, 0)


def each_plane(result, apply):
    def one(channel, carry):
        rows = pl.ds(pl.multiple_of(channel * NY, NY), NY)
        for inner in range(2):
            apply(channel, inner, result[rows, inner * NZ:(inner + 1) * NZ])
        return carry

    lax.fori_loop(0, GROUP, one, 0)


def kernel(
    fields_hbm, cotangent_hbm, weights_hbm, analysis_y_hbm, synthesis_y_hbm, synthesis_z_hbm,
    local_weight, analysis_z, analysis_x, synthesis_x,
    through_hbm, last, weight_part_hbm,
    fields, cotangent, weights, analysis_y, synthesis_y, synthesis_z,
    sent, got, grid, flat, linear, slope, through, packed, doubled, values, grads, modes, result,
    spread_map, spectra, both, weight_part,
    send_sem, recv_sem, own_sem, load_sem, store_sem, pack_sem, part_sem,
):
    me = lax.axis_index("slab")
    sample = lax.axis_index("batch")
    cells = [(slice(None), pl.ds(2 * pair, 2)) for pair in range(2)]
    loads = [
        pltpu.make_async_copy(source, target, load_sem.at[index])
        for index, (source, target) in enumerate((
            (analysis_y_hbm, analysis_y), (fields_hbm.at[cells[0]], fields.at[cells[0]]),
            (weights_hbm, weights), (fields_hbm.at[cells[1]], fields.at[cells[1]]),
            (synthesis_z_hbm, synthesis_z), (synthesis_y_hbm, synthesis_y),
            (cotangent_hbm, cotangent),
        ))
    ]
    for load in loads[:3]:
        load.start()
    barrier = pltpu.get_barrier_semaphore()

    def greet(step, carry):
        pl.semaphore_signal(
            barrier, inc=1, device_id=((me + step) % SLABS, sample), device_id_type=MESH
        )
        return carry

    lax.fori_loop(1, SLABS, greet, 0)
    for step in range(1, BATCHES):
        pl.semaphore_signal(
            barrier, inc=1, device_id=(me, (sample + step) % BATCHES), device_id_type=MESH
        )

    def send(turn, pair, target):
        pltpu.make_async_remote_copy(
            src_ref=sent.at[turn, pair, target],
            dst_ref=got.at[turn, pair, me],
            send_sem=send_sem.at[turn, pair],
            recv_sem=recv_sem.at[turn, pair],
            device_id=(target, sample),
            device_id_type=MESH,
        ).start()

    def keep(turn, pair):
        pltpu.make_async_copy(
            sent.at[turn, pair, me], got.at[turn, pair, me], own_sem.at[turn, pair]
        ).start()

    some = pl.ds(0, SLABS - 1)

    def wait_messages(turn, pair):
        pltpu.make_async_copy(
            sent.at[turn, pair, me], got.at[turn, pair, me], own_sem.at[turn, pair]
        ).wait()
        pltpu.make_async_copy(
            sent.at[turn, pair, some], got.at[turn, pair, some], recv_sem.at[turn, pair]
        ).wait()

    def receive(turn, pair):
        wait_messages(turn, pair)
        unpack(got.at[turn, pair], flat.at[pair])

    def analyse_y(source, pair):
        def step(group, carry):
            channels = pl.ds(group * GROUP, GROUP)
            planes = [
                source[channels, 2 * pair + inner].reshape(GROUP * NY, NZ) for inner in range(2)
            ]
            first = matmul(analysis_y[...], jnp.concatenate(planes, 1))
            first = first.reshape(2, MY, GROUP, 2 * NZ)
            for inner in range(2):
                row = pl.multiple_of(inner * C + group * GROUP, GROUP)
                for part in range(2):
                    grid[:, pl.ds(row, GROUP), part * NZ:(part + 1) * NZ] = first[
                        part, :, :, inner * NZ:(inner + 1) * NZ
                    ]
            return carry

        lax.fori_loop(0, GROUPS, step, 0)

    def analyse_z(turn, pair):
        left = lane_index((MZ, LANES)) < LANES // 2

        def transform(index):
            batch = [(me // 2 + index * 4 + inner) % MY for inner in range(4)]
            for two in (batch[:2], batch[2:]):
                first = jnp.concatenate([grid[ky] for ky in two], 0).astype(BF16)
                second = lax.dot_general(
                    analysis_z[...], first, (((1,), (1,)), ((), ())), preferred_element_type=F32
                )
                upper, lower = second[:MZ], second[MZ:]
                ready = (
                    jnp.where(left, upper, pltpu.roll(lower, LANES // 2, 1)),
                    jnp.where(left, pltpu.roll(upper, LANES // 2, 1), lower),
                )
                for ky, message in zip(two, ready):
                    for side in range(2):
                        sent[turn, pair, 2 * ky + side] = message[
                            ROWS * side:ROWS * (side + 1)
                        ].astype(BF16)
            return batch

        def step(index, carry):
            for ky in transform(index):
                for side in range(2):
                    send(turn, pair, 2 * ky + side)
            return carry

        for ky in transform(0)[1:]:
            for side in range(2):
                send(turn, pair, 2 * ky + side)
        send(turn, pair, me + 1 - 2 * (me % 2))
        keep(turn, pair)
        lax.fori_loop(1, MY // 4, step, 0)

    def analyse_x(target, scale):
        for block in range(BATCHES):
            parts = []
            for part in range(2):
                cells = []
                for pair in range(2):
                    rows = pl.ds(block * 2 + part, SLABS, stride=ROWS)
                    cells += split_cells(flat[pair, rows, :])
                parts.append(matmul(analysis_x[...], jnp.concatenate(cells, 0).astype(BF16)))
            real = parts[0][:MX] + parts[1][MX:]
            imag = parts[1][:MX] - parts[0][MX:]
            turned = jnp.concatenate([real, imag], 0).T
            held = [
                turned[2 * C * b:2 * C * b + C] + turned[2 * C * b + C:2 * C * (b + 1)]
                for b in range(HELD)
            ]
            pieces = [held[b][:, part * MX:(part + 1) * MX] for part in range(2) for b in range(HELD)]
            target[block] = jnp.concatenate(pieces, 1) * scale

    def synthesise_x(turn):
        for block in range(BATCHES):
            rounded = modes[block].astype(BF16).astype(F32)
            tall = []
            for b in range(HELD):
                piece = jnp.concatenate([
                    rounded[:, part * MODES + b * MX:part * MODES + (b + 1) * MX]
                    for part in range(2)
                ], 1)
                tall += [piece, piece]
            turned = jnp.concatenate(tall, 0).T
            real, imag = turned[:MX], turned[MX:]
            for part in range(2):
                pair = [real, -imag] if part == 0 else [imag, real]
                stacked = jnp.concatenate(split_cells(jnp.concatenate(pair, 0)), 0).astype(BF16)
                product = matmul(synthesis_x[...], stacked)
                for half in range(2):
                    rows = pl.ds(block * 2 + part, SLABS, stride=ROWS)
                    flat[half, rows, :] = product[half * SLABS:(half + 1) * SLABS]

        for half in range(2):
            def pack(index, carry, half=half):
                for inner in range(8):
                    target = index * 8 + inner
                    sent[turn, half, target] = flat[
                        half, pl.ds(pl.multiple_of(target * ROWS, ROWS), ROWS), :
                    ].astype(BF16)
                return carry

            def step(index, carry, half=half):
                for inner in range(1, 10):
                    send(turn, half, (me + index * 9 + inner) % SLABS)
                return carry

            lax.fori_loop(0, SLABS // 8, pack, 0)
            lax.fori_loop(0, SLABS // 9, step, 0)
            keep(turn, half)

    def pointwise(source, turned, target):
        spread_map[...] = spread(local_weight[...], turned)

        def step(index, carry):
            pair = (index // (NY // BAND)) * 2
            band = pl.ds(pl.multiple_of((index % (NY // BAND)) * BAND, BAND), BAND)
            columns = [source[:, pair + inner, band, :].reshape(C * BAND, NZ) for inner in range(2)]
            product = matmul(spread_map[...], jnp.concatenate(columns, 1))
            for inner in range(2):
                target[:, pair + inner, band, :] = product[
                    :, inner * NZ:(inner + 1) * NZ
                ].reshape(C, BAND, NZ).astype(target.dtype)
            return carry

        lax.fori_loop(0, 2 * (NY // BAND), step, 0)

    def weight_copy(step):
        return pltpu.make_async_remote_copy(
            src_ref=packed.at[sample],
            dst_ref=packed.at[sample],
            send_sem=pack_sem.at[0],
            recv_sem=pack_sem.at[1],
            device_id=(me, (sample + step) % BATCHES),
            device_id_type=MESH,
        )

    def pack_weights(index, carry):
        for inner in range(8):
            channel = index * 8 + inner
            pieces = [weights[part, channel].astype(F32) for part in range(2)]
            packed[sample, channel] = jnp.concatenate(pieces, 1).astype(BF16)
        return carry

    three = pl.ds(0, BATCHES - 1)
    lower = lane_index((C, LANES)) < MODES

    def swapped(block):
        return pltpu.roll(block, MODES, 1)

    def double_weights(channel, carry):
        for block in range(BATCHES):
            both = packed[block, channel].astype(F32)
            turned = swapped(both)
            doubled[block, 0, channel] = jnp.where(lower, both, turned)
            doubled[block, 1, channel] = jnp.where(lower, turned, both)
        return carry

    def mix():
        for block in range(BATCHES):
            turned = swapped(values[block])
            both[0, block] = jnp.where(lower, -turned, turned)

        def step(channel, totals):
            row = pl.ds(channel, 1)
            return tuple(
                totals[block]
                + doubled[block, 0, channel] * values[block, row, :]
                + doubled[block, 1, channel] * both[0, block, row, :]
                for block in range(BATCHES)
            )

        start = tuple(jnp.zeros((C, LANES), F32) for _ in range(BATCHES))
        totals = lax.fori_loop(0, C, step, start)
        for block in range(BATCHES):
            modes[block] = totals[block]

    def turned_grads(block):
        turned = swapped(grads[block])
        return jnp.where(lower, turned, -turned)

    def back_mix():
        for block in range(BATCHES):
            straight, other = grads[block], turned_grads(block)

            def step(channel, carry, block=block, straight=straight, other=other):
                product = (
                    doubled[block, 0, channel] * straight + doubled[block, 1, channel] * other
                )
                modes[block, pl.ds(channel, 1), :] = jnp.sum(product, 0, keepdims=True)
                return carry

            lax.fori_loop(0, C, step, 0)

    def spectrum_copy(kind, source, step):
        return pltpu.make_async_remote_copy(
            src_ref=source.at[(sample + step) % BATCHES],
            dst_ref=spectra.at[kind, sample],
            send_sem=part_sem.at[kind, 0],
            recv_sem=part_sem.at[kind, 1],
            device_id=(me, (sample + step) % BATCHES),
            device_id_type=MESH,
        )

    def share(kind, source):
        for step in range(1, BATCHES):
            spectrum_copy(kind, source, step).start()
        spectra[kind, sample] = source[sample]

    def weight_products():
        for kind in range(2):
            pltpu.make_async_copy(
                values.at[three], spectra.at[kind, three], part_sem.at[kind, 1]
            ).wait()
        straight, other = [], []
        for part in range(BATCHES):
            turned = swapped(spectra[0, part])
            both[0, part] = jnp.where(lower, spectra[0, part], turned)
            both[1, part] = jnp.where(lower, turned, spectra[0, part])
            turned = swapped(spectra[1, part])
            straight.append(spectra[1, part])
            other.append(jnp.where(lower, turned, -turned))

        def step(channel, carry):
            row = pl.ds(channel, 1)
            total = jnp.zeros((C, LANES), F32)
            for part in range(BATCHES):
                total = total + straight[part] * both[0, part, row, :]
                total = total + other[part] * both[1, part, row, :]
            weight_part[channel] = total
            return carry

        lax.fori_loop(0, C, step, 0)

    def forward_half(pair, carry):
        receive(1, pair)
        synthesise_z(flat.at[pair], grid, synthesis_z)

        def finish(group):
            def apply(offset, inner, part):
                place = (group * GROUP + offset, 2 * pair + inner)
                slopes = gelu_slope(linear[place] + part * SCALE_OUT)
                slope[place] = (cotangent[place].astype(F32) * slopes).astype(BF16)

            each_plane(result, apply)

        synthesise_y(grid, synthesis_y, result, finish)
        analyse_y(slope, pair)
        analyse_z(2, pair)
        return carry

    loads[0].wait()
    loads[1].wait()
    for load in loads[3:]:
        load.start()
    analyse_y(fields, 0)
    loads[2].wait()
    lax.fori_loop(0, C // 8, pack_weights, 0)
    pl.semaphore_wait(barrier, SLABS - 1 + BATCHES - 1)
    for step in range(1, BATCHES):
        weight_copy(step).start()
    analyse_z(0, 0)
    loads[3].wait()
    analyse_y(fields, 1)
    analyse_z(0, 1)
    pointwise(fields, True, linear)
    for load in loads[4:]:
        load.wait()
    pltpu.make_async_copy(packed.at[three], packed.at[three], pack_sem.at[1]).wait()
    lax.fori_loop(0, C, double_weights, 0)
    receive(0, 0)
    receive(0, 1)
    analyse_x(values, SCALE_IN)
    share(0, values)
    mix()
    synthesise_x(1)
    lax.fori_loop(0, 2, forward_half, 0)
    pointwise(slope, False, through)
    store = pltpu.make_async_copy(through, through_hbm, store_sem.at[0])
    store.start()
    receive(2, 0)
    receive(2, 1)
    analyse_x(grads, SCALE_OUT)
    share(1, grads)
    back_mix()
    synthesise_x(3)
    weight_products()
    part_store = pltpu.make_async_copy(weight_part, weight_part_hbm, store_sem.at[1])
    part_store.start()
    store.wait()
    part_store.wait()
    for pair in range(2):
        wait_messages(3, pair)
        last[pair] = got[3, pair]
    for turn in range(4):
        for pair in range(2):
            pltpu.make_async_copy(
                sent.at[turn, pair, some], got.at[turn, pair, some], send_sem.at[turn, pair]
            ).wait()
    pltpu.make_async_copy(packed.at[three], packed.at[three], pack_sem.at[0]).wait()
    for kind in range(2):
        pltpu.make_async_copy(
            values.at[three], spectra.at[kind, three], part_sem.at[kind, 0]
        ).wait()


def last_kernel(
    messages, synthesis_z, synthesis_y, through_hbm, field_grad_hbm,
    grid, flat, result, through, field_grad, load_sem, store_sem,
):
    def some(pair, group):
        return (pl.ds(group * GROUP, GROUP), pl.ds(2 * pair, 2))

    def load(pair, group):
        return pltpu.make_async_copy(
            through_hbm.at[some(pair, group)], through.at[some(pair, group)],
            load_sem.at[pair, group],
        )

    def store(pair, group):
        return pltpu.make_async_copy(
            field_grad.at[some(pair, group)], field_grad_hbm.at[some(pair, group)],
            store_sem.at[pair, group],
        )

    for pair in range(2):
        for group in range(GROUPS):
            load(pair, group).start()

    def half(pair, carry):
        unpack(messages.at[pair], flat)
        synthesise_z(flat, grid, synthesis_z)

        def finish(group):
            load(pair, group).wait()

            def apply(offset, inner, part):
                place = (group * GROUP + offset, 2 * pair + inner)
                field_grad[place] = (through[place].astype(F32) + part * SCALE_IN).astype(BF16)

            each_plane(result, apply)
            store(pair, group).start()

        synthesise_y(grid, synthesis_y, result, finish)
        return carry

    lax.fori_loop(0, 2, half, 0)
    for pair in range(2):
        for group in range(GROUPS):
            store(pair, group).wait()


def body(fields, cotangent, local_weight, spectral_weight):
    shape = (C, WIDTH, NY, NZ)
    analysis_y, synthesis_y, analysis_z, synthesis_z, analysis_x, synthesis_x = make_tables()
    far = (
        fields.reshape(shape), cotangent.reshape(shape), spectral_weight,
        analysis_y, synthesis_y, synthesis_z,
    )
    near = (local_weight, analysis_z, analysis_x, synthesis_x)
    in_vmem, anywhere = pl.BlockSpec(memory_space=pltpu.VMEM), pl.BlockSpec(memory_space=pl.ANY)
    field_shape = jax.ShapeDtypeStruct(shape, BF16)
    message_shape = jax.ShapeDtypeStruct((2, SLABS, ROWS, LANES), BF16)
    part_shape = jax.ShapeDtypeStruct((C, C, LANES), F32)
    grid_shape = (MY, 2 * C, 2 * NZ)
    through, messages, part = pl.pallas_call(
        kernel,
        out_shape=(field_shape, message_shape, part_shape),
        in_specs=[anywhere] * len(far) + [in_vmem] * len(near),
        out_specs=[anywhere, in_vmem, anywhere],
        scratch_shapes=[pltpu.VMEM(array.shape, BF16) for array in far] + [
            pltpu.VMEM((4, 2, SLABS, ROWS, LANES), BF16),
            pltpu.VMEM((4, 2, SLABS, ROWS, LANES), BF16),
            pltpu.VMEM(grid_shape, F32),
            pltpu.VMEM((2, SLABS * ROWS, LANES), F32),
            pltpu.VMEM(shape, F32),
            pltpu.VMEM(shape, BF16),
            pltpu.VMEM(shape, BF16),
            pltpu.VMEM((BATCHES, C, C, LANES), BF16),
            pltpu.VMEM((BATCHES, 2, C, C, LANES), F32),
            pltpu.VMEM((BATCHES, C, LANES), F32),
            pltpu.VMEM((BATCHES, C, LANES), F32),
            pltpu.VMEM((BATCHES, C, LANES), F32),
            pltpu.VMEM((GROUP * NY, 2 * NZ), F32),
            pltpu.VMEM((C * BAND, C * BAND), BF16),
            pltpu.VMEM((2, BATCHES, C, LANES), F32),
            pltpu.VMEM((2, BATCHES, C, LANES), F32),
            pltpu.VMEM(part_shape.shape, F32),
            pltpu.SemaphoreType.DMA((4, 2)),
            pltpu.SemaphoreType.DMA((4, 2)),
            pltpu.SemaphoreType.DMA((4, 2)),
            pltpu.SemaphoreType.DMA((len(far) + 1,)),
            pltpu.SemaphoreType.DMA((2,)),
            pltpu.SemaphoreType.DMA((2,)),
            pltpu.SemaphoreType.DMA((2, 2)),
        ],
        compiler_params=pltpu.CompilerParams(
            collective_id=0, has_side_effects=True, vmem_limit_bytes=60 << 20
        ),
    )(*far, *near)
    field_grad = pl.pallas_call(
        last_kernel,
        out_shape=field_shape,
        in_specs=[in_vmem] * 3 + [anywhere],
        out_specs=anywhere,
        scratch_shapes=[
            pltpu.VMEM(grid_shape, F32),
            pltpu.VMEM((SLABS * ROWS, LANES), F32),
            pltpu.VMEM((GROUP * NY, 2 * NZ), F32),
            pltpu.VMEM(shape, BF16),
            pltpu.VMEM(shape, BF16),
            pltpu.SemaphoreType.DMA((2, GROUPS)),
            pltpu.SemaphoreType.DMA((2, GROUPS)),
        ],
        compiler_params=pltpu.CompilerParams(vmem_limit_bytes=60 << 20),
    )(messages, synthesis_z, synthesis_y, through)
    weight_grad = jnp.stack([part[:, :, :MODES], part[:, :, MODES:]], 0)
    return (field_grad.reshape(fields.shape), weight_grad)


def solution(mesh):
    placed = (
        P("batch", None, "slab", None, None),
        P("batch", None, "slab", None, None),
        P(),
        P(None, None, None, ("slab", "batch")),
    )
    return jax.shard_map(
        body,
        mesh=mesh,
        in_specs=placed,
        out_specs=(P("batch", None, "slab", None, None), P(None, None, None, ("slab", "batch"))),
        check_vma=False,
    )
```

```python
import math

import jax
import jax.numpy as jnp
import ml_dtypes
import numpy as np
from jax import lax
from jax.experimental import pallas as pl
from jax.experimental.pallas import tpu as pltpu
from jax.sharding import PartitionSpec as P

C = 32
NX = 256
NY = 128
NZ = 128
MX = 32
MY = 32
MZ = 16
SLABS = 64
BATCHES = 4
WIDTH = NX // SLABS
HELD = 2
HIGH = MZ // HELD
MODES = HELD * MX
LANES = 2 * MODES
ROWS = 2 * BATCHES
GROUP = 8
GROUPS = C // GROUP
BAND = 16
SOME_KY = 8
AT_ONCE = 8
MESH = pl.DeviceIdType.MESH
F32 = jnp.float32
BF16 = jnp.bfloat16
SCALE_IN = 1.0 / math.sqrt(NX * NY * NZ)
SCALE_OUT = 1.0 / math.sqrt(MX * MY * MZ * C)


def wave_table(number, length, signed):
    numbers = np.arange(number)
    if signed:
        numbers = np.where(numbers < number // 2, numbers, numbers - number)
    phases = np.mod(numbers[:, None] * np.arange(length)[None, :], length).astype(np.float32)
    angles = phases * np.float32(2.0 * math.pi / length)
    return (np.cos(angles).astype(np.float32), np.sin(angles).astype(np.float32))


def make_tables():
    cos_y, sin_y = wave_table(MY, NY, True)
    cos_z, sin_z = wave_table(MZ, NZ, False)
    cos_x, sin_x = wave_table(MX, NX, True)
    eye = np.eye(GROUP, dtype=np.float32)
    pair_y = np.stack([cos_y, -sin_y])
    analysis_y = np.einsum("pky,ab->pkaby", pair_y, eye).reshape(2 * MY * GROUP, GROUP * NY)
    synthesis_y = np.einsum("pky,ab->aypkb", pair_y, eye).reshape(GROUP * NY, 2 * MY * GROUP)
    both_z = np.stack([np.stack([cos_z, sin_z], 1), np.stack([-sin_z, cos_z], 1)])
    both_z = both_z.reshape(2, HIGH, HELD, 2 * NZ)
    analysis_z = both_z.transpose(2, 1, 0, 3).reshape(2 * MZ, 2 * NZ)
    several = np.eye(SOME_KY, dtype=np.float32)
    synthesis_z = np.einsum("qhlw,ab->lahqbw", both_z, several)
    synthesis_z = synthesis_z.reshape(SOME_KY * 2 * MZ, SOME_KY * 2 * NZ)
    both_x = np.stack([cos_x, sin_x]).reshape(2, MX, SLABS, WIDTH).transpose(0, 1, 3, 2)
    analysis_x = both_x.reshape(2 * MX, WIDTH * SLABS)
    synthesis_x = both_x.reshape(2, MX, 2, 2, SLABS).transpose(2, 4, 3, 0, 1)
    synthesis_x = synthesis_x.reshape(2 * SLABS, 2 * 2 * MX)
    tables = (analysis_y, synthesis_y, analysis_z, synthesis_z, analysis_x, synthesis_x)
    return tuple(np.ascontiguousarray(table).astype(ml_dtypes.bfloat16) for table in tables)


def matmul(left, right):
    return jnp.dot(left, right, preferred_element_type=F32)


def gelu_slope(values):
    values = values.astype(BF16)
    size = jnp.abs(values)
    inverse = pl.reciprocal(1.0 + (0.3275911 / math.sqrt(2.0)) * size, approx=True)
    tail = 0.5 * 1.061405429 * inverse - 0.5 * 1.453152027
    tail = tail * inverse + 0.5 * 1.421413741
    tail = tail * inverse - 0.5 * 0.284496736
    tail = tail * inverse + 0.5 * 0.254829592
    tail = tail * inverse - size * (1.0 / math.sqrt(2.0 * math.pi))
    below = jnp.exp2((-0.5 / math.log(2.0)) * (values * values)) * tail
    return jnp.where(values >= 0.0, 1.0 - below, below)


def lane_index(shape):
    return lax.broadcasted_iota(jnp.int32, shape, len(shape) - 1)


def split_cells(value):
    second = (lane_index(value.shape) // C) % 2 == 1
    return [jnp.where(second, 0.0, value), jnp.where(second, value, 0.0)]


def spread(weight, turned):
    rows = C * BAND
    left = (
        lax.broadcasted_iota(jnp.int32, (rows, C), 0) // BAND
        == lax.broadcasted_iota(jnp.int32, (rows, C), 1)
    ).astype(F32).astype(BF16)
    right = (
        lax.broadcasted_iota(jnp.int32, (C, rows), 1) // BAND
        == lax.broadcasted_iota(jnp.int32, (C, rows), 0)
    ).astype(F32).astype(BF16)
    side = 1 if turned else 0
    tall = lax.dot_general(left, weight, (((1,), (side,)), ((), ())), preferred_element_type=F32)
    whole = matmul(tall.astype(BF16), right)
    same = (
        lax.broadcasted_iota(jnp.int32, (rows, rows), 0) % BAND
        == lax.broadcasted_iota(jnp.int32, (rows, rows), 1) % BAND
    )
    return jnp.where(same, whole, 0.0).astype(BF16)


def unpack(source, flat):
    def step(index, carry):
        for inner in range(8):
            tile = index * 8 + inner
            flat[pl.ds(pl.multiple_of(tile * ROWS, ROWS), ROWS), :] = source[tile].astype(F32)
        return carry

    lax.fori_loop(0, SLABS // 8, step, 0)


def synthesise_z(flat, grid, table):
    rows = SOME_KY * MZ
    half = LANES // 2
    batches = MY // SOME_KY
    blocks = []
    for batch in range(batches):
        turned = flat[pl.ds(batch * rows, rows), :].T
        blocks.append(jnp.concatenate([turned[:half], turned[half:]], 1))
    left = jnp.concatenate(blocks, 0).astype(BF16)
    for inner in range(SOME_KY):
        second = matmul(left, table[:, inner * 2 * NZ:(inner + 1) * 2 * NZ])
        for batch in range(batches):
            grid[batch * SOME_KY + inner] = second[batch * half:(batch + 1) * half]


def synthesise_y(grid, table, result, finish):
    def step(group, carry):
        columns = []
        for inner in range(2):
            row = pl.multiple_of(inner * C + group * GROUP, GROUP)
            halves = [
                grid[:, pl.ds(row, GROUP), part * NZ:(part + 1) * NZ].reshape(MY * GROUP, NZ)
                for part in range(2)
            ]
            columns.append(jnp.concatenate(halves, 0).astype(BF16))
        result[...] = matmul(table[...], jnp.concatenate(columns, 1))
        finish(group)
        return carry

    lax.fori_loop(0, GROUPS, step, 0)


def each_plane(result, apply):
    def one(channel, carry):
        rows = pl.ds(pl.multiple_of(channel * NY, NY), NY)
        for inner in range(2):
            apply(channel, inner, result[rows, inner * NZ:(inner + 1) * NZ])
        return carry

    lax.fori_loop(0, GROUP, one, 0)


def kernel(
    fields_hbm, cotangent_hbm, weights_hbm, analysis_y_hbm, synthesis_y_hbm, synthesis_z_hbm,
    local_weight, analysis_z, analysis_x, synthesis_x,
    through_hbm, last, weight_part_hbm,
    fields, cotangent, weights, analysis_y, synthesis_y, synthesis_z,
    sent, got, grid, flat, linear, slope, through, packed, doubled, values, grads, modes, result,
    spread_map, spectra, both, weight_part,
    send_sem, recv_sem, own_sem, load_sem, store_sem, pack_sem, part_sem,
):
    me = lax.axis_index("slab")
    sample = lax.axis_index("batch")
    cells = [(slice(None), pl.ds(2 * pair, 2)) for pair in range(2)]
    loads = [
        pltpu.make_async_copy(source, target, load_sem.at[index])
        for index, (source, target) in enumerate((
            (analysis_y_hbm, analysis_y), (fields_hbm.at[cells[0]], fields.at[cells[0]]),
            (weights_hbm, weights), (fields_hbm.at[cells[1]], fields.at[cells[1]]),
            (synthesis_z_hbm, synthesis_z), (synthesis_y_hbm, synthesis_y),
            (cotangent_hbm, cotangent),
        ))
    ]
    for load in loads[:3]:
        load.start()
    barrier = pltpu.get_barrier_semaphore()

    def greet(step, carry):
        pl.semaphore_signal(
            barrier, inc=1, device_id=((me + step) % SLABS, sample), device_id_type=MESH
        )
        return carry

    lax.fori_loop(1, SLABS, greet, 0)
    for step in range(1, BATCHES):
        pl.semaphore_signal(
            barrier, inc=1, device_id=(me, (sample + step) % BATCHES), device_id_type=MESH
        )

    def send(turn, pair, target):
        pltpu.make_async_remote_copy(
            src_ref=sent.at[turn, pair, target],
            dst_ref=got.at[turn, pair, me],
            send_sem=send_sem.at[turn, pair],
            recv_sem=recv_sem.at[turn, pair],
            device_id=(target, sample),
            device_id_type=MESH,
        ).start()

    def keep(turn, pair):
        pltpu.make_async_copy(
            sent.at[turn, pair, me], got.at[turn, pair, me], own_sem.at[turn, pair]
        ).start()

    some = pl.ds(0, SLABS - 1)

    def wait_messages(turn, pair):
        pltpu.make_async_copy(
            sent.at[turn, pair, me], got.at[turn, pair, me], own_sem.at[turn, pair]
        ).wait()
        pltpu.make_async_copy(
            sent.at[turn, pair, some], got.at[turn, pair, some], recv_sem.at[turn, pair]
        ).wait()

    def receive(turn, pair):
        wait_messages(turn, pair)
        unpack(got.at[turn, pair], flat.at[pair])

    def analyse_y(source, pair):
        def step(group, carry):
            channels = pl.ds(group * GROUP, GROUP)
            planes = [
                source[channels, 2 * pair + inner].reshape(GROUP * NY, NZ) for inner in range(2)
            ]
            first = matmul(analysis_y[...], jnp.concatenate(planes, 1))
            first = first.reshape(2, MY, GROUP, 2 * NZ)
            for inner in range(2):
                row = pl.multiple_of(inner * C + group * GROUP, GROUP)
                for part in range(2):
                    grid[:, pl.ds(row, GROUP), part * NZ:(part + 1) * NZ] = first[
                        part, :, :, inner * NZ:(inner + 1) * NZ
                    ]
            return carry

        lax.fori_loop(0, GROUPS, step, 0)

    def analyse_z(turn, pair):
        left = lane_index((MZ, LANES)) < LANES // 2

        def transform(index):
            batch = [(me // 2 + index * AT_ONCE + inner) % MY for inner in range(AT_ONCE)]
            for start in range(0, AT_ONCE, 2):
                two = batch[start:start + 2]
                first = jnp.concatenate([grid[ky] for ky in two], 0).astype(BF16)
                second = lax.dot_general(
                    analysis_z[...], first, (((1,), (1,)), ((), ())), preferred_element_type=F32
                )
                upper, lower = second[:MZ], second[MZ:]
                ready = (
                    jnp.where(left, upper, pltpu.roll(lower, LANES // 2, 1)),
                    jnp.where(left, pltpu.roll(upper, LANES // 2, 1), lower),
                )
                for ky, message in zip(two, ready):
                    for side in range(2):
                        sent[turn, pair, 2 * ky + side] = message[
                            ROWS * side:ROWS * (side + 1)
                        ].astype(BF16)
            return batch

        def leave(batch):
            for ky in batch:
                for side in range(2):
                    send(turn, pair, 2 * ky + side)

        ready = transform(0)[1:]
        for index in range(1, MY // AT_ONCE):
            later = transform(index)
            leave(ready)
            ready = later
        leave(ready)
        send(turn, pair, me + 1 - 2 * (me % 2))
        keep(turn, pair)

    def analyse_x(target, scale):
        for block in range(BATCHES):
            parts = []
            for part in range(2):
                cells = []
                for pair in range(2):
                    rows = pl.ds(block * 2 + part, SLABS, stride=ROWS)
                    cells += split_cells(flat[pair, rows, :])
                parts.append(matmul(analysis_x[...], jnp.concatenate(cells, 0).astype(BF16)))
            real = parts[0][:MX] + parts[1][MX:]
            imag = parts[1][:MX] - parts[0][MX:]
            turned = jnp.concatenate([real, imag], 0).T
            held = [
                turned[2 * C * b:2 * C * b + C] + turned[2 * C * b + C:2 * C * (b + 1)]
                for b in range(HELD)
            ]
            pieces = [held[b][:, part * MX:(part + 1) * MX] for part in range(2) for b in range(HELD)]
            target[block] = jnp.concatenate(pieces, 1) * scale

    def synthesise_x(turn):
        for block in range(BATCHES):
            rounded = modes[block].astype(BF16).astype(F32)
            tall = []
            for b in range(HELD):
                piece = jnp.concatenate([
                    rounded[:, part * MODES + b * MX:part * MODES + (b + 1) * MX]
                    for part in range(2)
                ], 1)
                tall += [piece, piece]
            turned = jnp.concatenate(tall, 0).T
            real, imag = turned[:MX], turned[MX:]
            for part in range(2):
                pair = [real, -imag] if part == 0 else [imag, real]
                stacked = jnp.concatenate(split_cells(jnp.concatenate(pair, 0)), 0).astype(BF16)
                product = matmul(synthesis_x[...], stacked)
                for half in range(2):
                    rows = pl.ds(block * 2 + part, SLABS, stride=ROWS)
                    flat[half, rows, :] = product[half * SLABS:(half + 1) * SLABS]

        for half in range(2):
            def pack(index, carry, half=half):
                for inner in range(8):
                    target = index * 8 + inner
                    sent[turn, half, target] = flat[
                        half, pl.ds(pl.multiple_of(target * ROWS, ROWS), ROWS), :
                    ].astype(BF16)
                return carry

            def step(index, carry, half=half):
                for inner in range(1, 10):
                    send(turn, half, (me + index * 9 + inner) % SLABS)
                return carry

            lax.fori_loop(0, SLABS // 8, pack, 0)
            lax.fori_loop(0, SLABS // 9, step, 0)
            keep(turn, half)

    def pointwise(source, turned, target):
        spread_map[...] = spread(local_weight[...], turned)

        def step(index, carry):
            pair = (index // (NY // BAND)) * 2
            band = pl.ds(pl.multiple_of((index % (NY // BAND)) * BAND, BAND), BAND)
            columns = [source[:, pair + inner, band, :].reshape(C * BAND, NZ) for inner in range(2)]
            product = matmul(spread_map[...], jnp.concatenate(columns, 1))
            for inner in range(2):
                target[:, pair + inner, band, :] = product[
                    :, inner * NZ:(inner + 1) * NZ
                ].reshape(C, BAND, NZ).astype(target.dtype)
            return carry

        lax.fori_loop(0, 2 * (NY // BAND), step, 0)

    def weight_copy(step):
        return pltpu.make_async_remote_copy(
            src_ref=packed.at[sample],
            dst_ref=packed.at[sample],
            send_sem=pack_sem.at[0],
            recv_sem=pack_sem.at[1],
            device_id=(me, (sample + step) % BATCHES),
            device_id_type=MESH,
        )

    def pack_weights(index, carry):
        for inner in range(8):
            channel = index * 8 + inner
            pieces = [weights[part, channel].astype(F32) for part in range(2)]
            packed[sample, channel] = jnp.concatenate(pieces, 1).astype(BF16)
        return carry

    three = pl.ds(0, BATCHES - 1)
    lower = lane_index((C, LANES)) < MODES

    def swapped(block):
        return pltpu.roll(block, MODES, 1)

    def double_weights(channel, carry):
        for block in range(BATCHES):
            both = packed[block, channel].astype(F32)
            turned = swapped(both)
            doubled[block, 0, channel] = jnp.where(lower, both, turned)
            doubled[block, 1, channel] = jnp.where(lower, turned, both)
        return carry

    def mix():
        for block in range(BATCHES):
            turned = swapped(values[block])
            both[0, block] = jnp.where(lower, -turned, turned)

        def step(channel, totals):
            row = pl.ds(channel, 1)
            return tuple(
                totals[block]
                + doubled[block, 0, channel] * values[block, row, :]
                + doubled[block, 1, channel] * both[0, block, row, :]
                for block in range(BATCHES)
            )

        start = tuple(jnp.zeros((C, LANES), F32) for _ in range(BATCHES))
        totals = lax.fori_loop(0, C, step, start)
        for block in range(BATCHES):
            modes[block] = totals[block]

    def turned_grads(block):
        turned = swapped(grads[block])
        return jnp.where(lower, turned, -turned)

    def back_mix():
        for block in range(BATCHES):
            straight, other = grads[block], turned_grads(block)

            def step(channel, carry, block=block, straight=straight, other=other):
                product = (
                    doubled[block, 0, channel] * straight + doubled[block, 1, channel] * other
                )
                modes[block, pl.ds(channel, 1), :] = jnp.sum(product, 0, keepdims=True)
                return carry

            lax.fori_loop(0, C, step, 0)

    def spectrum_copy(kind, source, step):
        return pltpu.make_async_remote_copy(
            src_ref=source.at[(sample + step) % BATCHES],
            dst_ref=spectra.at[kind, sample],
            send_sem=part_sem.at[kind, 0],
            recv_sem=part_sem.at[kind, 1],
            device_id=(me, (sample + step) % BATCHES),
            device_id_type=MESH,
        )

    def share(kind, source):
        for step in range(1, BATCHES):
            spectrum_copy(kind, source, step).start()
        spectra[kind, sample] = source[sample]

    def weight_products():
        for kind in range(2):
            pltpu.make_async_copy(
                values.at[three], spectra.at[kind, three], part_sem.at[kind, 1]
            ).wait()
        straight, other = [], []
        for part in range(BATCHES):
            turned = swapped(spectra[0, part])
            both[0, part] = jnp.where(lower, spectra[0, part], turned)
            both[1, part] = jnp.where(lower, turned, spectra[0, part])
            turned = swapped(spectra[1, part])
            straight.append(spectra[1, part])
            other.append(jnp.where(lower, turned, -turned))

        def step(channel, carry):
            row = pl.ds(channel, 1)
            total = jnp.zeros((C, LANES), F32)
            for part in range(BATCHES):
                total = total + straight[part] * both[0, part, row, :]
                total = total + other[part] * both[1, part, row, :]
            weight_part[channel] = total
            return carry

        lax.fori_loop(0, C, step, 0)

    def forward_half(pair, carry):
        receive(1, pair)
        synthesise_z(flat.at[pair], grid, synthesis_z)

        def finish(group):
            def apply(offset, inner, part):
                place = (group * GROUP + offset, 2 * pair + inner)
                slopes = gelu_slope(linear[place] + part * SCALE_OUT)
                slope[place] = cotangent[place] * slopes

            each_plane(result, apply)

        synthesise_y(grid, synthesis_y, result, finish)
        analyse_y(slope, pair)
        analyse_z(2, pair)
        return carry

    loads[0].wait()
    loads[1].wait()
    for load in loads[3:]:
        load.start()
    analyse_y(fields, 0)
    loads[2].wait()
    lax.fori_loop(0, C // 8, pack_weights, 0)
    pl.semaphore_wait(barrier, SLABS - 1 + BATCHES - 1)
    for step in range(1, BATCHES):
        weight_copy(step).start()
    analyse_z(0, 0)
    loads[3].wait()
    analyse_y(fields, 1)
    analyse_z(0, 1)
    pointwise(fields, True, linear)
    for load in loads[4:]:
        load.wait()
    pltpu.make_async_copy(packed.at[three], packed.at[three], pack_sem.at[1]).wait()
    lax.fori_loop(0, C, double_weights, 0)
    receive(0, 0)
    receive(0, 1)
    analyse_x(values, SCALE_IN)
    share(0, values)
    mix()
    synthesise_x(1)
    lax.fori_loop(0, 2, forward_half, 0)
    pointwise(slope, False, through)
    store = pltpu.make_async_copy(through, through_hbm, store_sem.at[0])
    store.start()
    receive(2, 0)
    receive(2, 1)
    analyse_x(grads, SCALE_OUT)
    share(1, grads)
    back_mix()
    synthesise_x(3)
    weight_products()
    part_store = pltpu.make_async_copy(weight_part, weight_part_hbm, store_sem.at[1])
    part_store.start()
    store.wait()
    part_store.wait()
    for pair in range(2):
        wait_messages(3, pair)
        last[pair] = got[3, pair]
    for turn in range(4):
        for pair in range(2):
            pltpu.make_async_copy(
                sent.at[turn, pair, some], got.at[turn, pair, some], send_sem.at[turn, pair]
            ).wait()
    pltpu.make_async_copy(packed.at[three], packed.at[three], pack_sem.at[0]).wait()
    for kind in range(2):
        pltpu.make_async_copy(
            values.at[three], spectra.at[kind, three], part_sem.at[kind, 0]
        ).wait()


def last_kernel(
    messages, synthesis_z, synthesis_y, through_hbm, field_grad_hbm,
    grid, flat, result, through, field_grad, load_sem, store_sem,
):
    def some(pair, group):
        return (pl.ds(group * GROUP, GROUP), pl.ds(2 * pair, 2))

    def load(pair, group):
        return pltpu.make_async_copy(
            through_hbm.at[some(pair, group)], through.at[some(pair, group)],
            load_sem.at[pair, group],
        )

    def store(pair, group):
        return pltpu.make_async_copy(
            field_grad.at[some(pair, group)], field_grad_hbm.at[some(pair, group)],
            store_sem.at[pair, group],
        )

    for pair in range(2):
        for group in range(GROUPS):
            load(pair, group).start()

    def half(pair, carry):
        unpack(messages.at[pair], flat)
        synthesise_z(flat, grid, synthesis_z)

        def finish(group):
            load(pair, group).wait()

            def apply(offset, inner, part):
                place = (group * GROUP + offset, 2 * pair + inner)
                field_grad[place] = (through[place].astype(F32) + part * SCALE_IN).astype(BF16)

            each_plane(result, apply)
            store(pair, group).start()

        synthesise_y(grid, synthesis_y, result, finish)
        return carry

    lax.fori_loop(0, 2, half, 0)
    for pair in range(2):
        for group in range(GROUPS):
            store(pair, group).wait()


def body(fields, cotangent, local_weight, spectral_weight):
    shape = (C, WIDTH, NY, NZ)
    analysis_y, synthesis_y, analysis_z, synthesis_z, analysis_x, synthesis_x = make_tables()
    far = (
        fields.reshape(shape), cotangent.reshape(shape), spectral_weight,
        analysis_y, synthesis_y, synthesis_z,
    )
    near = (local_weight, analysis_z, analysis_x, synthesis_x)
    in_vmem, anywhere = pl.BlockSpec(memory_space=pltpu.VMEM), pl.BlockSpec(memory_space=pl.ANY)
    field_shape = jax.ShapeDtypeStruct(shape, BF16)
    message_shape = jax.ShapeDtypeStruct((2, SLABS, ROWS, LANES), BF16)
    part_shape = jax.ShapeDtypeStruct((C, C, LANES), F32)
    grid_shape = (MY, 2 * C, 2 * NZ)
    through, messages, part = pl.pallas_call(
        kernel,
        out_shape=(field_shape, message_shape, part_shape),
        in_specs=[anywhere] * len(far) + [in_vmem] * len(near),
        out_specs=[anywhere, in_vmem, anywhere],
        scratch_shapes=[pltpu.VMEM(array.shape, BF16) for array in far] + [
            pltpu.VMEM((4, 2, SLABS, ROWS, LANES), BF16),
            pltpu.VMEM((4, 2, SLABS, ROWS, LANES), BF16),
            pltpu.VMEM(grid_shape, F32),
            pltpu.VMEM((2, SLABS * ROWS, LANES), F32),
            pltpu.VMEM(shape, F32),
            pltpu.VMEM(shape, BF16),
            pltpu.VMEM(shape, BF16),
            pltpu.VMEM((BATCHES, C, C, LANES), BF16),
            pltpu.VMEM((BATCHES, 2, C, C, LANES), F32),
            pltpu.VMEM((BATCHES, C, LANES), F32),
            pltpu.VMEM((BATCHES, C, LANES), F32),
            pltpu.VMEM((BATCHES, C, LANES), F32),
            pltpu.VMEM((GROUP * NY, 2 * NZ), F32),
            pltpu.VMEM((C * BAND, C * BAND), BF16),
            pltpu.VMEM((2, BATCHES, C, LANES), F32),
            pltpu.VMEM((2, BATCHES, C, LANES), F32),
            pltpu.VMEM(part_shape.shape, F32),
            pltpu.SemaphoreType.DMA((4, 2)),
            pltpu.SemaphoreType.DMA((4, 2)),
            pltpu.SemaphoreType.DMA((4, 2)),
            pltpu.SemaphoreType.DMA((len(far) + 1,)),
            pltpu.SemaphoreType.DMA((2,)),
            pltpu.SemaphoreType.DMA((2,)),
            pltpu.SemaphoreType.DMA((2, 2)),
        ],
        compiler_params=pltpu.CompilerParams(
            collective_id=0, has_side_effects=True, vmem_limit_bytes=60 << 20
        ),
    )(*far, *near)
    field_grad = pl.pallas_call(
        last_kernel,
        out_shape=field_shape,
        in_specs=[in_vmem] * 3 + [anywhere],
        out_specs=anywhere,
        scratch_shapes=[
            pltpu.VMEM(grid_shape, F32),
            pltpu.VMEM((SLABS * ROWS, LANES), F32),
            pltpu.VMEM((GROUP * NY, 2 * NZ), F32),
            pltpu.VMEM(shape, BF16),
            pltpu.VMEM(shape, BF16),
            pltpu.SemaphoreType.DMA((2, GROUPS)),
            pltpu.SemaphoreType.DMA((2, GROUPS)),
        ],
        compiler_params=pltpu.CompilerParams(vmem_limit_bytes=60 << 20),
    )(messages, synthesis_z, synthesis_y, through)
    weight_grad = jnp.stack([part[:, :, :MODES], part[:, :, MODES:]], 0)
    return (field_grad.reshape(fields.shape), weight_grad)


def solution(mesh):
    placed = (
        P("batch", None, "slab", None, None),
        P("batch", None, "slab", None, None),
        P(),
        P(None, None, None, ("slab", "batch")),
    )
    return jax.shard_map(
        body,
        mesh=mesh,
        in_specs=placed,
        out_specs=(P("batch", None, "slab", None, None), P(None, None, None, ("slab", "batch"))),
        check_vma=False,
    )
```

```python
import math

import jax
import jax.numpy as jnp
import ml_dtypes
import numpy as np
from jax import lax
from jax.experimental import pallas as pl
from jax.experimental.pallas import tpu as pltpu
from jax.sharding import PartitionSpec as P

C = 32
NX = 256
NY = 128
NZ = 128
MX = 32
MY = 32
MZ = 16
SLABS = 64
BATCHES = 4
WIDTH = NX // SLABS
HELD = 2
HIGH = MZ // HELD
MODES = HELD * MX
LANES = 2 * MODES
ROWS = 2 * BATCHES
GROUP = 8
GROUPS = C // GROUP
BAND = 16
SOME_KY = 8
AT_ONCE = 8
MESH = pl.DeviceIdType.MESH
F32 = jnp.float32
BF16 = jnp.bfloat16
SCALE_IN = 1.0 / math.sqrt(NX * NY * NZ)
SCALE_OUT = 1.0 / math.sqrt(MX * MY * MZ * C)


def wave_table(number, length, signed):
    numbers = np.arange(number)
    if signed:
        numbers = np.where(numbers < number // 2, numbers, numbers - number)
    phases = np.mod(numbers[:, None] * np.arange(length)[None, :], length).astype(np.float32)
    angles = phases * np.float32(2.0 * math.pi / length)
    return (np.cos(angles).astype(np.float32), np.sin(angles).astype(np.float32))


def make_tables():
    cos_y, sin_y = wave_table(MY, NY, True)
    cos_z, sin_z = wave_table(MZ, NZ, False)
    cos_x, sin_x = wave_table(MX, NX, True)
    eye = np.eye(GROUP, dtype=np.float32)
    pair_y = np.stack([cos_y, -sin_y])
    analysis_y = np.einsum("pky,ab->pkaby", pair_y, eye).reshape(2 * MY * GROUP, GROUP * NY)
    synthesis_y = np.einsum("pky,ab->aypkb", pair_y, eye).reshape(GROUP * NY, 2 * MY * GROUP)
    both_z = np.stack([np.stack([cos_z, sin_z], 1), np.stack([-sin_z, cos_z], 1)])
    both_z = both_z.reshape(2, HIGH, HELD, 2 * NZ)
    analysis_z = both_z.transpose(2, 1, 0, 3).reshape(2 * MZ, 2 * NZ)
    several = np.eye(SOME_KY, dtype=np.float32)
    synthesis_z = np.einsum("qhlw,ab->lahqbw", both_z, several)
    synthesis_z = synthesis_z.reshape(SOME_KY * 2 * MZ, SOME_KY * 2 * NZ)
    both_x = np.stack([cos_x, sin_x]).reshape(2, MX, SLABS, WIDTH).transpose(0, 1, 3, 2)
    analysis_x = both_x.reshape(2 * MX, WIDTH * SLABS)
    synthesis_x = both_x.reshape(2, MX, 2, 2, SLABS).transpose(2, 4, 3, 0, 1)
    synthesis_x = synthesis_x.reshape(2 * SLABS, 2 * 2 * MX)
    tables = (analysis_y, synthesis_y, analysis_z, synthesis_z, analysis_x, synthesis_x)
    return tuple(np.ascontiguousarray(table).astype(ml_dtypes.bfloat16) for table in tables)


def matmul(left, right):
    return jnp.dot(left, right, preferred_element_type=F32)


def gelu_slope(values):
    values = values.astype(BF16)
    size = jnp.abs(values)
    inverse = pl.reciprocal(1.0 + (0.3275911 / math.sqrt(2.0)) * size, approx=True)
    tail = 0.5 * 1.061405429 * inverse - 0.5 * 1.453152027
    tail = tail * inverse + 0.5 * 1.421413741
    tail = tail * inverse - 0.5 * 0.284496736
    tail = tail * inverse + 0.5 * 0.254829592
    tail = tail * inverse - size * (1.0 / math.sqrt(2.0 * math.pi))
    below = jnp.exp2((-0.5 / math.log(2.0)) * (values * values)) * tail
    return jnp.where(values >= 0.0, 1.0 - below, below)


def lane_index(shape):
    return lax.broadcasted_iota(jnp.int32, shape, len(shape) - 1)


def split_cells(value):
    second = (lane_index(value.shape) // C) % 2 == 1
    return [jnp.where(second, 0.0, value), jnp.where(second, value, 0.0)]


def spread(weight, turned):
    rows = C * BAND
    left = (
        lax.broadcasted_iota(jnp.int32, (rows, C), 0) // BAND
        == lax.broadcasted_iota(jnp.int32, (rows, C), 1)
    ).astype(F32).astype(BF16)
    right = (
        lax.broadcasted_iota(jnp.int32, (C, rows), 1) // BAND
        == lax.broadcasted_iota(jnp.int32, (C, rows), 0)
    ).astype(F32).astype(BF16)
    side = 1 if turned else 0
    tall = lax.dot_general(left, weight, (((1,), (side,)), ((), ())), preferred_element_type=F32)
    whole = matmul(tall.astype(BF16), right)
    same = (
        lax.broadcasted_iota(jnp.int32, (rows, rows), 0) % BAND
        == lax.broadcasted_iota(jnp.int32, (rows, rows), 1) % BAND
    )
    return jnp.where(same, whole, 0.0).astype(BF16)


def unpack(source, flat):
    def step(index, carry):
        for inner in range(8):
            tile = index * 8 + inner
            flat[pl.ds(pl.multiple_of(tile * ROWS, ROWS), ROWS), :] = source[tile].astype(F32)
        return carry

    lax.fori_loop(0, SLABS // 8, step, 0)


def synthesise_z(flat, grid, table):
    rows = SOME_KY * MZ
    half = LANES // 2
    batches = MY // SOME_KY
    blocks = []
    for batch in range(batches):
        turned = flat[pl.ds(batch * rows, rows), :].T
        blocks.append(jnp.concatenate([turned[:half], turned[half:]], 1))
    left = jnp.concatenate(blocks, 0).astype(BF16)
    for inner in range(SOME_KY):
        second = matmul(left, table[:, inner * 2 * NZ:(inner + 1) * 2 * NZ])
        for batch in range(batches):
            grid[batch * SOME_KY + inner] = second[batch * half:(batch + 1) * half]


def synthesise_y(grid, table, result, finish):
    def step(group, carry):
        columns = []
        for inner in range(2):
            row = pl.multiple_of(inner * C + group * GROUP, GROUP)
            halves = [
                grid[:, pl.ds(row, GROUP), part * NZ:(part + 1) * NZ].reshape(MY * GROUP, NZ)
                for part in range(2)
            ]
            columns.append(jnp.concatenate(halves, 0).astype(BF16))
        result[...] = matmul(table[...], jnp.concatenate(columns, 1))
        finish(group)
        return carry

    lax.fori_loop(0, GROUPS, step, 0)


def each_plane(result, apply):
    def one(channel, carry):
        rows = pl.ds(pl.multiple_of(channel * NY, NY), NY)
        for inner in range(2):
            apply(channel, inner, result[rows, inner * NZ:(inner + 1) * NZ])
        return carry

    lax.fori_loop(0, GROUP, one, 0)


def kernel(
    fields_hbm, cotangent_hbm, weights_hbm, analysis_y_hbm, synthesis_y_hbm, synthesis_z_hbm,
    local_weight, analysis_z, analysis_x, synthesis_x,
    through_hbm, last, weight_part_hbm,
    fields, cotangent, weights, analysis_y, synthesis_y, synthesis_z,
    sent, got, grid, flat, linear, slope, through, packed, doubled, values, grads, modes, result,
    spread_map, spectra, both, weight_part,
    send_sem, recv_sem, own_sem, load_sem, store_sem, pack_sem, part_sem,
):
    me = lax.axis_index("slab")
    sample = lax.axis_index("batch")
    cells = [(slice(None), pl.ds(2 * pair, 2)) for pair in range(2)]
    loads = [
        pltpu.make_async_copy(source, target, load_sem.at[index])
        for index, (source, target) in enumerate((
            (analysis_y_hbm, analysis_y), (fields_hbm.at[cells[0]], fields.at[cells[0]]),
            (weights_hbm, weights), (fields_hbm.at[cells[1]], fields.at[cells[1]]),
            (synthesis_z_hbm, synthesis_z), (synthesis_y_hbm, synthesis_y),
            (cotangent_hbm, cotangent),
        ))
    ]
    for load in loads[:3]:
        load.start()
    barrier = pltpu.get_barrier_semaphore()

    def greet(step, carry):
        pl.semaphore_signal(
            barrier, inc=1, device_id=((me + step) % SLABS, sample), device_id_type=MESH
        )
        return carry

    lax.fori_loop(1, SLABS, greet, 0)
    for step in range(1, BATCHES):
        pl.semaphore_signal(
            barrier, inc=1, device_id=(me, (sample + step) % BATCHES), device_id_type=MESH
        )

    def send(turn, pair, target):
        pltpu.make_async_remote_copy(
            src_ref=sent.at[turn, pair, target],
            dst_ref=got.at[turn, pair, me],
            send_sem=send_sem.at[turn, pair],
            recv_sem=recv_sem.at[turn, pair],
            device_id=(target, sample),
            device_id_type=MESH,
        ).start()

    def keep(turn, pair):
        pltpu.make_async_copy(
            sent.at[turn, pair, me], got.at[turn, pair, me], own_sem.at[turn, pair]
        ).start()

    some = pl.ds(0, SLABS - 1)

    def wait_messages(turn, pair):
        pltpu.make_async_copy(
            sent.at[turn, pair, me], got.at[turn, pair, me], own_sem.at[turn, pair]
        ).wait()
        pltpu.make_async_copy(
            sent.at[turn, pair, some], got.at[turn, pair, some], recv_sem.at[turn, pair]
        ).wait()

    def receive(turn, pair):
        wait_messages(turn, pair)
        unpack(got.at[turn, pair], flat.at[pair])

    def analyse_y(source, pair):
        def step(group, carry):
            channels = pl.ds(group * GROUP, GROUP)
            planes = [
                source[channels, 2 * pair + inner].reshape(GROUP * NY, NZ) for inner in range(2)
            ]
            first = matmul(analysis_y[...], jnp.concatenate(planes, 1))
            first = first.reshape(2, MY, GROUP, 2 * NZ)
            for inner in range(2):
                row = pl.multiple_of(inner * C + group * GROUP, GROUP)
                for part in range(2):
                    grid[:, pl.ds(row, GROUP), part * NZ:(part + 1) * NZ] = first[
                        part, :, :, inner * NZ:(inner + 1) * NZ
                    ]
            return carry

        lax.fori_loop(0, GROUPS, step, 0)

    def analyse_z(turn, pair):
        left = lane_index((MZ, LANES)) < LANES // 2

        def transform(index):
            batch = [(me // 2 + index * AT_ONCE + inner) % MY for inner in range(AT_ONCE)]
            for start in range(0, AT_ONCE, 2):
                two = batch[start:start + 2]
                first = jnp.concatenate([grid[ky] for ky in two], 0).astype(BF16)
                second = lax.dot_general(
                    analysis_z[...], first, (((1,), (1,)), ((), ())), preferred_element_type=F32
                )
                upper, lower = second[:MZ], second[MZ:]
                ready = (
                    jnp.where(left, upper, pltpu.roll(lower, LANES // 2, 1)),
                    jnp.where(left, pltpu.roll(upper, LANES // 2, 1), lower),
                )
                for ky, message in zip(two, ready):
                    for side in range(2):
                        sent[turn, pair, 2 * ky + side] = message[
                            ROWS * side:ROWS * (side + 1)
                        ].astype(BF16)
            return batch

        def leave(batch):
            for ky in batch:
                for side in range(2):
                    send(turn, pair, 2 * ky + side)

        ready = transform(0)[1:]
        for index in range(1, MY // AT_ONCE):
            later = transform(index)
            leave(ready)
            ready = later
        leave(ready)
        send(turn, pair, me + 1 - 2 * (me % 2))
        keep(turn, pair)

    def analyse_x(target, scale):
        for block in range(BATCHES):
            parts = []
            for part in range(2):
                cells = []
                for pair in range(2):
                    rows = pl.ds(block * 2 + part, SLABS, stride=ROWS)
                    cells += split_cells(flat[pair, rows, :])
                parts.append(matmul(analysis_x[...], jnp.concatenate(cells, 0).astype(BF16)))
            real = parts[0][:MX] + parts[1][MX:]
            imag = parts[1][:MX] - parts[0][MX:]
            turned = jnp.concatenate([real, imag], 0).T
            held = [
                turned[2 * C * b:2 * C * b + C] + turned[2 * C * b + C:2 * C * (b + 1)]
                for b in range(HELD)
            ]
            pieces = [held[b][:, part * MX:(part + 1) * MX] for part in range(2) for b in range(HELD)]
            target[block] = jnp.concatenate(pieces, 1) * scale

    def synthesise_x(turn):
        for block in range(BATCHES):
            rounded = modes[block].astype(BF16).astype(F32)
            tall = []
            for b in range(HELD):
                piece = jnp.concatenate([
                    rounded[:, part * MODES + b * MX:part * MODES + (b + 1) * MX]
                    for part in range(2)
                ], 1)
                tall += [piece, piece]
            turned = jnp.concatenate(tall, 0).T
            real, imag = turned[:MX], turned[MX:]
            for part in range(2):
                pair = [real, -imag] if part == 0 else [imag, real]
                stacked = jnp.concatenate(split_cells(jnp.concatenate(pair, 0)), 0).astype(BF16)
                product = matmul(synthesis_x[...], stacked)
                for half in range(2):
                    rows = pl.ds(block * 2 + part, SLABS, stride=ROWS)
                    flat[half, rows, :] = product[half * SLABS:(half + 1) * SLABS]

        for half in range(2):
            def pack(index, carry, half=half):
                for inner in range(8):
                    target = index * 8 + inner
                    sent[turn, half, target] = flat[
                        half, pl.ds(pl.multiple_of(target * ROWS, ROWS), ROWS), :
                    ].astype(BF16)
                return carry

            def step(index, carry, half=half):
                for inner in range(1, 10):
                    send(turn, half, (me + index * 9 + inner) % SLABS)
                return carry

            lax.fori_loop(0, SLABS // 8, pack, 0)
            lax.fori_loop(0, SLABS // 9, step, 0)
            keep(turn, half)

    def pointwise(source, turned, target):
        spread_map[...] = spread(local_weight[...], turned)

        def step(index, carry):
            pair = (index // (NY // BAND)) * 2
            band = pl.ds(pl.multiple_of((index % (NY // BAND)) * BAND, BAND), BAND)
            columns = [source[:, pair + inner, band, :].reshape(C * BAND, NZ) for inner in range(2)]
            product = matmul(spread_map[...], jnp.concatenate(columns, 1))
            for inner in range(2):
                target[:, pair + inner, band, :] = product[
                    :, inner * NZ:(inner + 1) * NZ
                ].reshape(C, BAND, NZ).astype(target.dtype)
            return carry

        lax.fori_loop(0, 2 * (NY // BAND), step, 0)

    def weight_copy(step):
        return pltpu.make_async_remote_copy(
            src_ref=packed.at[sample],
            dst_ref=packed.at[sample],
            send_sem=pack_sem.at[0],
            recv_sem=pack_sem.at[1],
            device_id=(me, (sample + step) % BATCHES),
            device_id_type=MESH,
        )

    def pack_weights(index, carry):
        for inner in range(8):
            channel = index * 8 + inner
            pieces = [weights[part, channel].astype(F32) for part in range(2)]
            packed[sample, channel] = jnp.concatenate(pieces, 1).astype(BF16)
        return carry

    three = pl.ds(0, BATCHES - 1)
    lower = lane_index((C, LANES)) < MODES

    def swapped(block):
        return pltpu.roll(block, MODES, 1)

    def double_weights(channel, carry):
        for block in range(BATCHES):
            both = packed[block, channel].astype(F32)
            turned = swapped(both)
            doubled[block, 0, channel] = jnp.where(lower, both, turned)
            doubled[block, 1, channel] = jnp.where(lower, turned, both)
        return carry

    def mix():
        for block in range(BATCHES):
            turned = swapped(values[block])
            both[0, block] = jnp.where(lower, -turned, turned)

        def step(channel, totals):
            row = pl.ds(channel, 1)
            return tuple(
                totals[block]
                + doubled[block, 0, channel] * values[block, row, :]
                + doubled[block, 1, channel] * both[0, block, row, :]
                for block in range(BATCHES)
            )

        start = tuple(jnp.zeros((C, LANES), F32) for _ in range(BATCHES))
        totals = lax.fori_loop(0, C, step, start)
        for block in range(BATCHES):
            modes[block] = totals[block]

    def turned_grads(block):
        turned = swapped(grads[block])
        return jnp.where(lower, turned, -turned)

    def back_mix():
        for block in range(BATCHES):
            straight, other = grads[block], turned_grads(block)

            def step(channel, carry, block=block, straight=straight, other=other):
                product = (
                    doubled[block, 0, channel] * straight + doubled[block, 1, channel] * other
                )
                modes[block, pl.ds(channel, 1), :] = jnp.sum(product, 0, keepdims=True)
                return carry

            lax.fori_loop(0, C, step, 0)

    def spectrum_copy(kind, source, step):
        return pltpu.make_async_remote_copy(
            src_ref=source.at[(sample + step) % BATCHES],
            dst_ref=spectra.at[kind, sample],
            send_sem=part_sem.at[kind, 0],
            recv_sem=part_sem.at[kind, 1],
            device_id=(me, (sample + step) % BATCHES),
            device_id_type=MESH,
        )

    def share(kind, source):
        for step in range(1, BATCHES):
            spectrum_copy(kind, source, step).start()
        spectra[kind, sample] = source[sample]

    def weight_products():
        for kind in range(2):
            pltpu.make_async_copy(
                values.at[three], spectra.at[kind, three], part_sem.at[kind, 1]
            ).wait()
        straight, other = [], []
        for part in range(BATCHES):
            turned = swapped(spectra[0, part])
            both[0, part] = jnp.where(lower, spectra[0, part], turned)
            both[1, part] = jnp.where(lower, turned, spectra[0, part])
            turned = swapped(spectra[1, part])
            straight.append(spectra[1, part])
            other.append(jnp.where(lower, turned, -turned))

        def step(channel, carry):
            row = pl.ds(channel, 1)
            total = jnp.zeros((C, LANES), F32)
            for part in range(BATCHES):
                total = total + straight[part] * both[0, part, row, :]
                total = total + other[part] * both[1, part, row, :]
            weight_part[channel] = total
            return carry

        lax.fori_loop(0, C, step, 0)

    def forward_half(pair, carry):
        receive(1, pair)
        synthesise_z(flat.at[pair], grid, synthesis_z)

        def finish(group):
            def apply(offset, inner, part):
                place = (group * GROUP + offset, 2 * pair + inner)
                slopes = gelu_slope(linear[place] + part * SCALE_OUT)
                slope[place] = cotangent[place] * slopes

            each_plane(result, apply)

        synthesise_y(grid, synthesis_y, result, finish)
        analyse_y(slope, pair)
        analyse_z(2, pair)
        return carry

    loads[0].wait()
    loads[1].wait()
    for load in loads[3:]:
        load.start()
    analyse_y(fields, 0)
    loads[2].wait()
    lax.fori_loop(0, C // 8, pack_weights, 0)
    pl.semaphore_wait(barrier, SLABS - 1 + BATCHES - 1)
    for step in range(1, BATCHES):
        weight_copy(step).start()
    analyse_z(0, 0)
    loads[3].wait()
    analyse_y(fields, 1)
    analyse_z(0, 1)
    pointwise(fields, True, linear)
    for load in loads[4:]:
        load.wait()
    pltpu.make_async_copy(packed.at[three], packed.at[three], pack_sem.at[1]).wait()
    lax.fori_loop(0, C, double_weights, 0)
    receive(0, 0)
    receive(0, 1)
    analyse_x(values, SCALE_IN)
    mix()
    synthesise_x(1)
    share(0, values)
    lax.fori_loop(0, 2, forward_half, 0)
    pointwise(slope, False, through)
    store = pltpu.make_async_copy(through, through_hbm, store_sem.at[0])
    store.start()
    receive(2, 0)
    receive(2, 1)
    analyse_x(grads, SCALE_OUT)
    back_mix()
    synthesise_x(3)
    share(1, grads)
    weight_products()
    part_store = pltpu.make_async_copy(weight_part, weight_part_hbm, store_sem.at[1])
    part_store.start()
    store.wait()
    part_store.wait()
    for pair in range(2):
        wait_messages(3, pair)
        last[pair] = got[3, pair]
    for turn in range(4):
        for pair in range(2):
            pltpu.make_async_copy(
                sent.at[turn, pair, some], got.at[turn, pair, some], send_sem.at[turn, pair]
            ).wait()
    pltpu.make_async_copy(packed.at[three], packed.at[three], pack_sem.at[0]).wait()
    for kind in range(2):
        pltpu.make_async_copy(
            values.at[three], spectra.at[kind, three], part_sem.at[kind, 0]
        ).wait()


def last_kernel(
    messages, synthesis_z, synthesis_y, through_hbm, field_grad_hbm,
    grid, flat, result, through, field_grad, load_sem, store_sem,
):
    def some(pair, group):
        return (pl.ds(group * GROUP, GROUP), pl.ds(2 * pair, 2))

    def load(pair, group):
        return pltpu.make_async_copy(
            through_hbm.at[some(pair, group)], through.at[some(pair, group)],
            load_sem.at[pair, group],
        )

    def store(pair, group):
        return pltpu.make_async_copy(
            field_grad.at[some(pair, group)], field_grad_hbm.at[some(pair, group)],
            store_sem.at[pair, group],
        )

    for pair in range(2):
        for group in range(GROUPS):
            load(pair, group).start()

    def half(pair, carry):
        unpack(messages.at[pair], flat)
        synthesise_z(flat, grid, synthesis_z)

        def finish(group):
            load(pair, group).wait()

            def apply(offset, inner, part):
                place = (group * GROUP + offset, 2 * pair + inner)
                field_grad[place] = (through[place].astype(F32) + part * SCALE_IN).astype(BF16)

            each_plane(result, apply)
            store(pair, group).start()

        synthesise_y(grid, synthesis_y, result, finish)
        return carry

    lax.fori_loop(0, 2, half, 0)
    for pair in range(2):
        for group in range(GROUPS):
            store(pair, group).wait()


def body(fields, cotangent, local_weight, spectral_weight):
    shape = (C, WIDTH, NY, NZ)
    analysis_y, synthesis_y, analysis_z, synthesis_z, analysis_x, synthesis_x = make_tables()
    far = (
        fields.reshape(shape), cotangent.reshape(shape), spectral_weight,
        analysis_y, synthesis_y, synthesis_z,
    )
    near = (local_weight, analysis_z, analysis_x, synthesis_x)
    in_vmem, anywhere = pl.BlockSpec(memory_space=pltpu.VMEM), pl.BlockSpec(memory_space=pl.ANY)
    field_shape = jax.ShapeDtypeStruct(shape, BF16)
    message_shape = jax.ShapeDtypeStruct((2, SLABS, ROWS, LANES), BF16)
    part_shape = jax.ShapeDtypeStruct((C, C, LANES), F32)
    grid_shape = (MY, 2 * C, 2 * NZ)
    through, messages, part = pl.pallas_call(
        kernel,
        out_shape=(field_shape, message_shape, part_shape),
        in_specs=[anywhere] * len(far) + [in_vmem] * len(near),
        out_specs=[anywhere, in_vmem, anywhere],
        scratch_shapes=[pltpu.VMEM(array.shape, BF16) for array in far] + [
            pltpu.VMEM((4, 2, SLABS, ROWS, LANES), BF16),
            pltpu.VMEM((4, 2, SLABS, ROWS, LANES), BF16),
            pltpu.VMEM(grid_shape, F32),
            pltpu.VMEM((2, SLABS * ROWS, LANES), F32),
            pltpu.VMEM(shape, F32),
            pltpu.VMEM(shape, BF16),
            pltpu.VMEM(shape, BF16),
            pltpu.VMEM((BATCHES, C, C, LANES), BF16),
            pltpu.VMEM((BATCHES, 2, C, C, LANES), F32),
            pltpu.VMEM((BATCHES, C, LANES), F32),
            pltpu.VMEM((BATCHES, C, LANES), F32),
            pltpu.VMEM((BATCHES, C, LANES), F32),
            pltpu.VMEM((GROUP * NY, 2 * NZ), F32),
            pltpu.VMEM((C * BAND, C * BAND), BF16),
            pltpu.VMEM((2, BATCHES, C, LANES), F32),
            pltpu.VMEM((2, BATCHES, C, LANES), F32),
            pltpu.VMEM(part_shape.shape, F32),
            pltpu.SemaphoreType.DMA((4, 2)),
            pltpu.SemaphoreType.DMA((4, 2)),
            pltpu.SemaphoreType.DMA((4, 2)),
            pltpu.SemaphoreType.DMA((len(far) + 1,)),
            pltpu.SemaphoreType.DMA((2,)),
            pltpu.SemaphoreType.DMA((2,)),
            pltpu.SemaphoreType.DMA((2, 2)),
        ],
        compiler_params=pltpu.CompilerParams(
            collective_id=0, has_side_effects=True, vmem_limit_bytes=60 << 20
        ),
    )(*far, *near)
    field_grad = pl.pallas_call(
        last_kernel,
        out_shape=field_shape,
        in_specs=[in_vmem] * 3 + [anywhere],
        out_specs=anywhere,
        scratch_shapes=[
            pltpu.VMEM(grid_shape, F32),
            pltpu.VMEM((SLABS * ROWS, LANES), F32),
            pltpu.VMEM((GROUP * NY, 2 * NZ), F32),
            pltpu.VMEM(shape, BF16),
            pltpu.VMEM(shape, BF16),
            pltpu.SemaphoreType.DMA((2, GROUPS)),
            pltpu.SemaphoreType.DMA((2, GROUPS)),
        ],
        compiler_params=pltpu.CompilerParams(vmem_limit_bytes=60 << 20),
    )(messages, synthesis_z, synthesis_y, through)
    weight_grad = jnp.stack([part[:, :, :MODES], part[:, :, MODES:]], 0)
    return (field_grad.reshape(fields.shape), weight_grad)


def solution(mesh):
    placed = (
        P("batch", None, "slab", None, None),
        P("batch", None, "slab", None, None),
        P(),
        P(None, None, None, ("slab", "batch")),
    )
    return jax.shard_map(
        body,
        mesh=mesh,
        in_specs=placed,
        out_specs=(P("batch", None, "slab", None, None), P(None, None, None, ("slab", "batch"))),
        check_vma=False,
    )
```
